128 devices in a mesh: gx: 8 (over y, core), gy: 16 (over z, x).
Axes of the slice: x: 4, y: 4, z: 4, core: 2. Of those that a mesh axis runs over, the one named last changes fastest.
Arguments:
- features: bfloat16 [128, 256, 96, 128], P('gx', 'gy'), may hold values from -160 to 160
- cotangent: bfloat16 [128, 256, 96, 128], P('gx', 'gy'), may hold values from -6 to 6
- weight: bfloat16 [27, 96, 96], replicated, may hold values from -0.125 to 0.125
- bn_gain: float32 [96], replicated, may hold values from 0.5 to 2
- bn_shift: float32 [96], replicated, may hold values from -3 to 3
- voxel_mask: int32 [128, 256, 128], P('gx', 'gy'), may hold values 0 or 1
- brick_live: int32 [8, 16, 8], P('gx', 'gy'), may hold values from 0 to 1, as said below
Outputs:
- input_grad: bfloat16 [128, 256, 96, 128], P('gx', 'gy')
- weight_grad: float32 [27, 96, 96], replicated
- gain_grad: float32 [96], replicated
- shift_grad: float32 [96], replicated
The draws below stay inside these ranges and needn't reach their ends.
Inputs may be any that keep to these rules, and one draw needn't show every extreme that they name: `brick_live`: along gy, the two tiles of one gx index whose gy indices differ by 8 hold exactly 2 live bricks together. In every gx index, the tiles with gy index 0 and 1 hold 1 each, and so do those with gy index 8 and 9, whose live bricks stand at the same vertical positions. At least one tile with gy index 2 to 7 holds 2.
All inputs are finite; a program needn't handle non-finite values. No bound on the sum of `voxel_mask` on one device may be relied on, other than what follows from the above.
Results may differ from the reference program's by a relative error of at most 0.0049.
Values may be sent and summed in bfloat16 or wider, within the bound.
No kernel may reach another device: no remote copies, remote signals or barrier semaphores. Data moves between devices by JAX's collectives and lax.ppermute only.
A program may use at most 256 MiB of HBM per device.

```python
import math
import jax
import jax.numpy as jnp
from jax import lax

C = 96
BRICK = 16
BZ = 8
MOST_LIVE = 2
NBX = 8
NBY = 16
NX = 128
NY = 256
NZ = 128


def draw_features(key, part):
    key = jax.random.fold_in(key, 11)
    key_values, key_scales = jax.random.split(key)
    values = jnp.clip(jax.random.normal(key_values, (NX, NY, C, NZ), jnp.float32), -5.0, 5.0)
    scales = jnp.exp(jax.random.uniform(key_scales, (C,), jnp.float32, 0.0, math.log(10.0)))
    along_x = jnp.arange(NX, dtype=jnp.float32) / max(NX - 1, 1)
    along_y = jnp.arange(NY, dtype=jnp.float32) / max(NY - 1, 1)
    position_gain = jnp.exp(0.5 * math.log(3.0) * (along_x[:, None] + along_y[None, :]))
    return (values * position_gain[:, :, None, None] * scales[None, None, :, None]).astype(jnp.bfloat16)


def draw_brick_live(key, part):
    key = jax.random.fold_in(key, 5)
    key_counts, key_force, key_order = jax.random.split(key, 3)
    half_row = NBY // 2
    counts = jax.random.randint(key_counts, (NBX, half_row), 0, MOST_LIVE + 1)
    forced = jax.random.randint(key_force, (NBX, 1), 2, half_row)
    columns = jnp.arange(half_row)[None, :]
    counts = jnp.where(columns == forced, MOST_LIVE, counts)
    counts = jnp.where(columns < 2, MOST_LIVE // 2, counts)
    counts = jnp.concatenate([counts, MOST_LIVE - counts], axis=1)
    scores = jax.random.randint(key_order, (NBX, NBY, BZ), 0, 1 << 20) * BZ + jnp.arange(BZ)[None, None, :]
    scores = scores.at[:, half_row + 1].set(scores[:, half_row])
    brick_rank = jnp.argsort(jnp.argsort(scores, axis=2), axis=2)
    return (brick_rank < counts[:, :, None]).astype(jnp.int32)


def place_ends(result, stream_key, low, high):
    dims = result.shape
    spot = [jax.random.randint(jax.random.fold_in(stream_key, axis), (), 0, dims[axis]) for axis in range(len(dims))]
    result = result.at[tuple(spot)].set(low)
    longest = dims.index(max(dims))
    spot[longest] = (spot[longest] + 1) % dims[longest]
    return result.at[tuple(spot)].set(high)


def block_scale(key, extent, cuts, least, top_value):
    factor_of = 1.0
    for position, shards_of in cuts:
        heights = jax.random.uniform(jax.random.fold_in(jax.random.fold_in(key, 6), position), (shards_of,), jnp.float32, least / len(cuts), top_value / len(cuts))
        factor_of = factor_of * jnp.repeat(jnp.exp(heights), extent[position] // shards_of).reshape((-1,) + (1,) * (len(extent) - 1 - position))
    return factor_of


def bell_draw(rng, dims, scale, limit, pieces=(), kind=jnp.bfloat16):
    level = block_scale(rng, dims, pieces, -0.22, 0.18) if pieces else 1.0
    result = jax.random.normal(rng, dims, jnp.float32) * scale * level
    return jnp.minimum(jnp.maximum(result, -limit), limit).astype(kind)


def setup_inputs(seed: int = 0) -> dict:
    keys = jax.random.split(jax.random.key(seed), 8)
    features = draw_features(jax.random.fold_in(keys[7], 71), 0)
    cotangent = bell_draw(keys[1], (NX, NY, C, NZ), 1.0, 6.0, ((0, 8), (1, 16)))
    weight = bell_draw(keys[2], (27, C, C), (27 * C) ** -0.5, 0.125)
    bn_gain = jnp.clip(jnp.exp(jax.random.uniform(keys[3], (C,), jnp.float32, math.log(0.5), math.log(2.0))), 0.5, 2.0)
    bn_shift = bell_draw(keys[4], (C,), 0.7, 3.0, (), jnp.float32)
    voxel_mask = place_ends((jax.random.randint(keys[5], (NX, NY, NZ), 0, 3) < 1).astype(jnp.int32), jax.random.fold_in(keys[5], 1), 0, 1)
    brick_live = draw_brick_live(jax.random.fold_in(keys[7], 71), 0)
    return {"features": features, "cotangent": cotangent, "weight": weight, "bn_gain": bn_gain, "bn_shift": bn_shift, "voxel_mask": voxel_mask, "brick_live": brick_live}


def unfold(padded_brick, brick_edge):
    shifted = [padded_brick[off_x:off_x + brick_edge, off_y:off_y + brick_edge, :, off_z:off_z + brick_edge] for off_x in range(3) for off_y in range(3) for off_z in range(3)]
    stacked = jnp.stack(shifted, 0)
    return jnp.transpose(stacked, (1, 2, 4, 0, 3)).reshape(brick_edge ** 3, 27 * padded_brick.shape[2])

def reference(features, cotangent, weight, bn_gain, bn_shift, voxel_mask, brick_live):
    live_total = NBX * NBY * MOST_LIVE // 2
    live_flags = brick_live.reshape(-1)
    chosen = jnp.argsort(1 - live_flags, stable=True)[:live_total].astype(jnp.int32)
    row_x = (chosen // (NBY * BZ)).astype(jnp.int32)
    row_y = (chosen // BZ % NBY).astype(jnp.int32)
    row_z = (chosen % BZ).astype(jnp.int32)
    zero_start = jnp.zeros((), jnp.int32)
    expanded = jnp.repeat(jnp.repeat(jnp.repeat(brick_live, BRICK, axis=0), BRICK, axis=1), BRICK, axis=2)
    mask_grid = (voxel_mask * expanded).astype(jnp.float32)
    masked = jnp.where(mask_grid[:, :, None, :] > 0, features, jnp.zeros_like(features))
    widened = jnp.pad(masked, ((1, 1), (1, 1), (0, 0), (1, 1)))
    weight_rows = weight.reshape(27 * C, C)
    weight_back = jnp.transpose(weight[::-1], (0, 2, 1)).reshape(27 * C, C)
    brick_ids = jnp.arange(live_total, dtype=jnp.int32)

    def cut_padded(values_grid, brick_index):
        starts = (row_x[brick_index] * BRICK, row_y[brick_index] * BRICK, zero_start, row_z[brick_index] * BRICK)
        return lax.dynamic_slice(values_grid, starts, (BRICK + 2, BRICK + 2, C, BRICK + 2))

    def cut_rows(brick_index):
        starts = (row_x[brick_index] * BRICK, row_y[brick_index] * BRICK, zero_start, row_z[brick_index] * BRICK)
        brick_piece = lax.dynamic_slice(cotangent, starts, (BRICK, BRICK, C, BRICK))
        return jnp.transpose(brick_piece, (0, 1, 3, 2)).reshape(BRICK ** 3, C)

    def cut_mask(brick_index):
        starts = (row_x[brick_index] * BRICK, row_y[brick_index] * BRICK, row_z[brick_index] * BRICK)
        return lax.dynamic_slice(mask_grid, starts, (BRICK, BRICK, BRICK)).reshape(BRICK ** 3)

    def forward_one(brick_index):
        return jnp.dot(unfold(cut_padded(widened, brick_index), BRICK), weight_rows, preferred_element_type=jnp.float32)
    preact = lax.map(forward_one, brick_ids)
    grad_rows = lax.map(cut_rows, brick_ids).astype(jnp.float32)
    mask_rows = lax.map(cut_mask, brick_ids)[:, :, None]
    voxels = jnp.sum(mask_grid)
    sum_pre = lax.optimization_barrier(jnp.sum(mask_rows * preact, axis=(0, 1)))
    sum_sq = lax.optimization_barrier(jnp.sum(mask_rows * preact * preact, axis=(0, 1)))
    bn_mean = sum_pre / voxels
    bn_var = sum_sq / voxels - bn_mean * bn_mean
    inv_std = lax.rsqrt(bn_var + 1e-05)
    normed = (preact - bn_mean) * inv_std
    zed = bn_gain * normed + bn_shift
    sigma = jax.nn.sigmoid(zed)
    grad_z = mask_rows * grad_rows * (sigma * (1.0 + zed * (1.0 - sigma)))
    sum_grad = lax.optimization_barrier(jnp.sum(grad_z, axis=(0, 1)))
    sum_cross = lax.optimization_barrier(jnp.sum(grad_z * normed, axis=(0, 1)))
    grad_pre = (mask_rows * bn_gain * inv_std * (grad_z - sum_grad / voxels - normed * sum_cross / voxels)).astype(jnp.bfloat16)

    def weight_step(running, brick_index):
        columns = unfold(cut_padded(widened, brick_index), BRICK)
        term = lax.dot_general(columns, grad_pre[brick_index], (((0,), (0,)), ((), ())), preferred_element_type=jnp.float32)
        return (running + term, None)
    weight_total, unused = lax.scan(weight_step, jnp.zeros((27 * C, C), jnp.float32), brick_ids)
    scale = 1.0 / jnp.sqrt(voxels)

    def scatter_bricks(values_grid, bricks):

        def place_one(brick_index, current):
            brick_piece = jnp.transpose(bricks[brick_index].reshape(BRICK, BRICK, BRICK, C), (0, 1, 3, 2))
            starts = (row_x[brick_index] * BRICK, row_y[brick_index] * BRICK, zero_start, row_z[brick_index] * BRICK)
            return lax.dynamic_update_slice(current, brick_piece, starts)
        return lax.fori_loop(0, live_total, place_one, values_grid)
    grad_grid = scatter_bricks(jnp.zeros(features.shape, jnp.bfloat16), grad_pre)
    widened_grad = jnp.pad(grad_grid, ((1, 1), (1, 1), (0, 0), (1, 1)))

    def backward_one(brick_index):
        product = jnp.dot(unfold(cut_padded(widened_grad, brick_index), BRICK), weight_back, preferred_element_type=jnp.float32)
        return product.astype(jnp.bfloat16)
    input_bricks = lax.map(backward_one, brick_ids)
    input_tile = scatter_bricks(jnp.zeros(features.shape, jnp.bfloat16), input_bricks)
    input_grad = jnp.where(mask_grid[:, :, None, :] > 0, input_tile, jnp.zeros_like(input_tile))
    return (input_grad, (weight_total * scale).reshape(27, C, C), sum_cross * scale, sum_grad * scale)
```

```python
import functools

import jax
import jax.numpy as jnp
from jax import lax
from jax.experimental import pallas as pl
from jax.experimental.pallas import tpu as pltpu
from jax.sharding import PartitionSpec as P

B = 16
C = 96
NB = 8
W2 = 512
ROWS = 20 * C
EDGE = C + 16
F32 = jnp.float32
BF16 = jnp.bfloat16
AXES = ("gx", "gy")


def params(mib=56):
    return pltpu.CompilerParams(vmem_limit_bytes=mib * 1024 * 1024)


def vmem():
    return pl.BlockSpec(memory_space=pltpu.VMEM)


def smem():
    return pl.BlockSpec(memory_space=pltpu.SMEM)


def iota(shape, dim):
    return lax.broadcasted_iota(jnp.int32, shape, dim)


def slots(live_ref):
    first = jnp.int32(-1)
    second = jnp.int32(-1)
    for j in reversed(range(NB)):
        on = live_ref[0, 0, j] > 0
        second = jnp.where(on, first, second)
        first = jnp.where(on, jnp.int32(j), first)
    ids = (jnp.maximum(first, 0), jnp.maximum(second, 0))
    return ids, (first >= 0, second >= 0)


def wrap(shift):
    return jnp.bitwise_and(shift + 256, 127)


def pack_tiles(load, ids):
    group = iota((C, 128), 1) // B
    tiles = []
    for s in range(2):
        for h in range(2):
            acc = None
            for j in range(8):
                r = pltpu.roll(load(h * 8 + j), wrap(16 * j - 16 * ids[s]), 1)
                acc = r if j == 0 else jnp.where(group == j, r, acc)
            tiles.append(acc)
    return tiles


def emit_faces(x, tiles, ids, faces):
    x0, x1, y0, y1, c00, c01, c10, c11 = faces
    group = iota((C, 128), 1) // B
    zero = jnp.zeros((C, 128), BF16)

    def side(face, low, high):
        for k in range(4):
            face[0:C, k * 128 : (k + 1) * 128] = tiles[k]
        low[0:C, :] = jnp.where(
            group == 0, tiles[0], jnp.where(group == 1, pltpu.roll(tiles[2], 16, 1), zero)
        )
        high[0:C, :] = jnp.where(
            group == 0,
            pltpu.roll(tiles[1], 16, 1),
            jnp.where(group == 1, pltpu.roll(tiles[3], 32, 1), zero),
        )

    @pl.when(x == 0)
    def _():
        side(x0, c00, c01)
        halves = [
            jnp.full((16, 256), 1.0, F32) * ids[s].astype(F32) for s in range(2)
        ]
        for face in (x0, x1, y0, y1):
            for s in range(2):
                face[C:EDGE, s * 256 : (s + 1) * 256] = halves[s].astype(BF16)
        mixed = jnp.where(
            iota((16, 128), 1) < B, ids[0].astype(F32), ids[1].astype(F32)
        ).astype(BF16)
        for face in (c00, c01, c10, c11):
            face[C:EDGE, :] = mixed

    @pl.when(x == B - 1)
    def _():
        side(x1, c10, c11)

    spot = lax.rem(x, 8)
    half = x // 8
    for face, base, off in ((y0, 0, 0), (y1, 1, 112)):
        for s in range(2):
            r = pltpu.roll(tiles[2 * s + base], wrap(16 * spot - off), 1)
            lanes = pl.ds(pl.multiple_of(s * 256 + half * 128, 128), 128)
            face[0:C, lanes] = jnp.where(group == spot, r, face[0:C, lanes])


FACES = [jax.ShapeDtypeStruct((EDGE, W2), BF16)] * 4 + [
    jax.ShapeDtypeStruct((EDGE, 128), BF16)
] * 4


def pack_features_kernel(live_ref, feat_ref, mask_ref, out_ref, live_out, *faces):
    x = pl.program_id(0)
    ids, valid = slots(live_ref)
    tiles = pack_tiles(lambda y: feat_ref[0, y], ids)
    cells = mask_ref[0].astype(F32)
    pick = iota((8, 128), 1) // B == iota((8, 128), 0)
    for s in range(2):
        keep = valid[s].astype(F32)
        for h in range(2):
            r = pltpu.roll(cells[h * 8 : (h + 1) * 8], wrap(-16 * ids[s]), 1)
            r = pltpu.roll(r, 0, 1, stride=16, stride_axis=0)
            row = jnp.sum(jnp.where(pick, r, 0.0), axis=0, keepdims=True) * keep
            k = 2 * s + h
            live_out[0, :, k * 128 : (k + 1) * 128] = row
            tiles[k] = tiles[k] * row.astype(BF16)
            out_ref[:, k * 128 : (k + 1) * 128] = tiles[k]
    emit_faces(x, tiles, ids, faces)


def whole(shape):
    return pl.BlockSpec(shape, lambda *a: (0,) * len(shape))


def pack_features(live, features, mask):
    return pl.pallas_call(
        pack_features_kernel,
        grid=(B,),
        in_specs=[
            smem(),
            pl.BlockSpec((1, B, C, 128), lambda x: (x, 0, 0, 0)),
            pl.BlockSpec((1, B, 128), lambda x: (x, 0, 0)),
        ],
        out_specs=[
            pl.BlockSpec((C, W2), lambda x: (x + 2, 0)),
            pl.BlockSpec((1, 1, W2), lambda x: (x, 0, 0)),
        ]
        + [whole(f.shape) for f in FACES],
        out_shape=[
            jax.ShapeDtypeStruct((ROWS, W2), BF16),
            jax.ShapeDtypeStruct((B, 1, W2), F32),
        ]
        + FACES,
        compiler_params=params(),
        name="pack_features",
    )(live, features, mask)


def pack_plain_kernel(live_ref, feat_ref, out_ref):
    ids, _ = slots(live_ref)
    tiles = pack_tiles(lambda y: feat_ref[0, y], ids)
    for k in range(4):
        out_ref[:, k * 128 : (k + 1) * 128] = tiles[k]


def pack_plain(live, values):
    return pl.pallas_call(
        pack_plain_kernel,
        grid=(B,),
        in_specs=[smem(), pl.BlockSpec((1, B, C, 128), lambda x: (x, 0, 0, 0))],
        out_specs=pl.BlockSpec((C, W2), lambda x: (x, 0)),
        out_shape=jax.ShapeDtypeStruct((B * C, W2), BF16),
        compiler_params=params(),
        name="pack_cotangent",
    )(live, values)


def exchange(faces):
    nx, ny = lax.axis_size("gx"), lax.axis_size("gy")

    def move(values, dx, dy):
        pairs = [
            (i * ny + j, (i + dx) * ny + j + dy)
            for i in range(nx)
            for j in range(ny)
            if 0 <= i + dx < nx and 0 <= j + dy < ny
        ]
        return lax.ppermute(values, AXES, pairs)

    x0, x1, y0, y1, c00, c01, c10, c11 = faces
    return (
        move(x1, 1, 0),
        move(x0, -1, 0),
        move(y1, 0, 1),
        move(y0, 0, -1),
        move(c11, 1, 1),
        move(c10, 1, -1),
        move(c01, -1, 1),
        move(c00, -1, -1),
    )


def assemble(ids, body, halo, ext, rows_ref):
    xm, xp, ym, yp, cmm, cmp_, cpm, cpp = halo
    group = iota((C, 128), 1) // B
    wide = iota((C, 384), 1)
    deep = jnp.bitwise_and(wide, 15)
    zero = jnp.zeros((C, 128), BF16)

    def matched(ref, s, d):
        total = None
        for t in range(2):
            lanes = slice(t * 256, (t + 1) * 256)
            tag = ref[C : C + 1, lanes].astype(F32)
            hit = jnp.where(tag == (ids[s] + d).astype(F32), 1.0, 0.0).astype(BF16)
            part = ref[0:C, lanes] * hit
            total = part if total is None else total + part
        return total

    def matched_corner(ref, s, d):
        tag = ref[C : C + 1, :].astype(F32)
        hit = jnp.where(tag == (ids[s] + d).astype(F32), 1.0, 0.0).astype(BF16)
        part = ref[0:C, :] * hit
        return jnp.where(group == 0, part + pltpu.roll(part, 112, 1), zero)

    def finish(i, s, planes):
        here, under, over = planes[1], planes[0], planes[2]
        lanes = slice(s * 384, (s + 1) * 384)
        ext[i, 1, :, lanes] = here
        ext[i, 0, :, lanes] = jnp.where(
            deep == 0, pltpu.roll(under, 384 - 15, 1), pltpu.roll(here, 1, 1)
        )
        ext[i, 2, :, lanes] = jnp.where(
            deep == 15, pltpu.roll(over, 15, 1), pltpu.roll(here, 383, 1)
        )

    for s in range(2):
        for way, ref in ((0, ym), (1, yp)):
            for d in (-1, 0, 1):
                rows_ref[s, way, d + 1] = matched(ref, s, d)
        for i, side, low, high in ((0, xm, cmm, cmp_), (17, xp, cpm, cpp)):
            planes = []
            for d in (-1, 0, 1):
                tail = matched_corner(high, s, d) + pltpu.roll(matched_corner(low, s, d), 112, 1)
                planes.append(jnp.concatenate([matched(side, s, d), tail], axis=1))
            finish(i, s, planes)

    after = (ids[1] == ids[0] + 1).astype(F32)

    def plane(x, carry):
        spot = lax.rem(x, 8)
        half = pl.ds(pl.multiple_of((x // 8) * 128, 128), 128)
        rows = pl.ds(pl.multiple_of((x + 2) * C, C), C)
        flag = jnp.full((1, 256), 1.0, F32) * after
        flag = flag.astype(BF16)
        for s in range(2):
            here = body[rows, s * 256 : (s + 1) * 256]
            other = body[rows, (1 - s) * 256 : (2 - s) * 256] * flag
            none = jnp.zeros((C, 256), BF16)
            centre = (none, here, other) if s == 0 else (other, here, none)
            planes = []
            for d in range(3):
                up = pltpu.roll(rows_ref[s, 1, d, :, half], wrap(-16 * spot), 1)
                down = pltpu.roll(rows_ref[s, 0, d, :, half], wrap(112 - 16 * spot), 1)
                tail = jnp.where(group == 0, up, jnp.where(group == 7, down, zero))
                planes.append(jnp.concatenate([centre[d], tail], axis=1))
            finish(x + 1, s, planes)
        return carry

    lax.fori_loop(0, B, plane, 0)


def fill_columns(ext, i, cols):
    for dz in range(3):
        for s in range(2):
            values = ext[i, dz, :, s * 384 : (s + 1) * 384]
            for dy in range(3):
                moved = values if dy == 1 else pltpu.roll(values, 16 if dy == 0 else 368, 1)
                k = dy * 3 + dz
                cols[k * C : (k + 1) * C, s * 256 : (s + 1) * 256] = moved[:, 0:256]


ASSEMBLY = [
    pltpu.VMEM((18, 3, C, 768), BF16),
    pltpu.VMEM((2, 2, 3, C, 256), BF16),
    pltpu.VMEM((9 * C, W2), BF16),
]


def convolve(weight_ref, ext, cols, sums):
    sums[...] = jnp.zeros_like(sums)

    def step(i, carry):
        fill_columns(ext, i, cols)
        part = jnp.dot(weight_ref[...], cols[...], preferred_element_type=F32)
        rows = pl.ds(pl.multiple_of(i * C, C), 3 * C)
        sums[rows, :] += part
        return carry

    lax.fori_loop(0, 18, step, 0)


def fold(values):
    return (values[:, 0:128] + values[:, 128:256]) + (values[:, 256:384] + values[:, 384:512])


def to_row(column_tile):
    column = jnp.sum(column_tile, axis=1, keepdims=True)
    diag = iota((C, 128), 0) == iota((C, 128), 1)
    return jnp.sum(jnp.where(diag, column, 0.0), axis=0, keepdims=True)


def to_column(row):
    diag = iota((C, 128), 0) == iota((C, 128), 1)
    return jnp.sum(jnp.where(diag, row, 0.0), axis=1, keepdims=True)


def forward_kernel(live_ref, body, *refs):
    halo, (weight_ref, mask_ref, pre_ref, stat_ref, ext, rows_ref, cols) = refs[:8], refs[8:]
    ids, _ = slots(live_ref)
    assemble(ids, body, halo, ext, rows_ref)
    convolve(weight_ref, ext, cols, pre_ref)

    def stat(x, carry):
        total, square, count = carry
        rows = pl.ds(pl.multiple_of((x + 2) * C, C), C)
        values = pre_ref[rows, :]
        mask = mask_ref[x]
        held = values * mask
        return total + fold(held), square + fold(held * values), count + mask

    total, square, count = lax.fori_loop(
        0,
        B,
        stat,
        (jnp.zeros((C, 128), F32), jnp.zeros((C, 128), F32), jnp.zeros((1, W2), F32)),
    )
    stat_ref[...] = jnp.zeros_like(stat_ref)
    stat_ref[0:1, :] = to_row(total)
    stat_ref[1:2, :] = to_row(square)
    stat_ref[2:3, :] = jnp.full((1, 128), 1.0, F32) * jnp.sum(count)


def forward(live, body, halo, weight, mask):
    return pl.pallas_call(
        forward_kernel,
        in_specs=[smem()] + [vmem()] * 11,
        out_specs=[vmem()] * 2,
        out_shape=[
            jax.ShapeDtypeStruct((ROWS, W2), F32),
            jax.ShapeDtypeStruct((8, 128), F32),
        ],
        scratch_shapes=ASSEMBLY,
        compiler_params=params(),
        name="forward",
    )(live, body, *halo, weight, mask)


def moments(stat_ref):
    total = jnp.sum(stat_ref[...], axis=0)
    voxels = total[2:3, :]
    mean = total[0:1, :] / voxels
    var = total[1:2, :] / voxels - mean * mean
    return voxels, mean, lax.rsqrt(var + 1e-05)


def slope_kernel(stat_ref, pre_ref, cot_ref, mask_ref, gain_ref, shift_ref, gz_ref, out_ref):
    voxels, mean, inv = moments(stat_ref)
    mean = to_column(mean)
    inv = to_column(inv)
    gain = to_column(gain_ref[...])
    shift = to_column(shift_ref[...])

    def step(x, carry):
        total, cross = carry
        rows = pl.ds(pl.multiple_of((x + 2) * C, C), C)
        own = pl.ds(pl.multiple_of(x * C, C), C)
        normed = (pre_ref[rows, :] - mean) * inv
        zed = gain * normed + shift
        sig = 1.0 / (1.0 + jnp.exp(-zed))
        gz = mask_ref[x] * cot_ref[own, :].astype(F32) * (sig * (1.0 + zed * (1.0 - sig)))
        gz_ref[own, :] = gz
        return total + fold(gz), cross + fold(gz * normed)

    total, cross = lax.fori_loop(
        0, B, step, (jnp.zeros((C, 128), F32), jnp.zeros((C, 128), F32))
    )
    out_ref[...] = jnp.zeros_like(out_ref)
    out_ref[0:1, :] = to_row(total)
    out_ref[1:2, :] = to_row(cross)


def slope(stats, pre, cot, mask, gain, shift):
    return pl.pallas_call(
        slope_kernel,
        in_specs=[vmem()] * 6,
        out_specs=[vmem()] * 2,
        out_shape=[
            jax.ShapeDtypeStruct((B * C, W2), F32),
            jax.ShapeDtypeStruct((8, 128), F32),
        ],
        compiler_params=params(),
        name="slope",
    )(stats, pre, cot, mask, gain, shift)


def pre_grad_kernel(
    live_ref, stat_ref, stat2_ref, pre_ref, gz_ref, mask_ref, gain_ref, out_ref, small_ref, *faces
):
    ids, _ = slots(live_ref)
    voxels, mean, inv = moments(stat_ref)
    total = jnp.sum(stat2_ref[...], axis=0)
    root = 1.0 / jnp.sqrt(voxels)
    small_ref[...] = jnp.zeros_like(small_ref)
    small_ref[0:1, :] = total[1:2, :] * root
    small_ref[1:2, :] = total[0:1, :] * root
    small_ref[2:3, :] = root
    scale = to_column(gain_ref[...] * inv)
    first = to_column(total[0:1, :] / voxels)
    second = to_column(total[1:2, :] / voxels)
    mean = to_column(mean)
    inv = to_column(inv)
    for q in (0, 1, 18, 19):
        out_ref[q * C : (q + 1) * C, :] = jnp.zeros((C, W2), BF16)

    def step(x, carry):
        rows = pl.ds(pl.multiple_of((x + 2) * C, C), C)
        own = pl.ds(pl.multiple_of(x * C, C), C)
        tiles = []
        for k in range(4):
            lanes = slice(k * 128, (k + 1) * 128)
            normed = (pre_ref[rows, lanes] - mean) * inv
            tile = (
                mask_ref[x][:, lanes] * scale * (gz_ref[own, lanes] - first - normed * second)
            ).astype(BF16)
            out_ref[rows, lanes] = tile
            tiles.append(tile)
        emit_faces(x, tiles, ids, faces)
        return carry

    lax.fori_loop(0, B, step, 0)


def pre_grad(live, stats, stats2, pre, gz, mask, gain):
    return pl.pallas_call(
        pre_grad_kernel,
        in_specs=[smem()] + [vmem()] * 6,
        out_specs=[vmem()] * 10,
        out_shape=[
            jax.ShapeDtypeStruct((ROWS, W2), BF16),
            jax.ShapeDtypeStruct((8, 128), F32),
        ]
        + FACES,
        compiler_params=params(),
        name="pre_grad",
    )(live, stats, stats2, pre, gz, mask, gain)


def weight_kernel(live_ref, body, *refs):
    halo, (grad_ref, out_ref, ext, rows_ref, cols, total) = refs[:8], refs[8:]
    ids, _ = slots(live_ref)
    assemble(ids, body, halo, ext, rows_ref)
    total[...] = jnp.zeros_like(total)

    def step(i, carry):
        fill_columns(ext, i, cols)
        rows = pl.ds(pl.multiple_of(i * C, C), 3 * C)
        total[...] += lax.dot_general(
            grad_ref[rows, :], cols[...], (((1,), (1,)), ((), ())), preferred_element_type=F32
        )
        return carry

    lax.fori_loop(0, 18, step, 0)
    for j in range(6):
        out_ref[j * 288 : (j + 1) * 288, :] = total[:, j * 128 : (j + 1) * 128]
    out_ref[6 * 288 : 2048, :] = jnp.zeros((2048 - 6 * 288, 128), F32)
    out_ref[6 * 288 : 7 * 288, 0:96] = total[:, 768:864]


def weight_terms(live, body, halo, grad):
    return pl.pallas_call(
        weight_kernel,
        in_specs=[smem()] + [vmem()] * 10,
        out_specs=vmem(),
        out_shape=jax.ShapeDtypeStruct((2048, 128), F32),
        scratch_shapes=ASSEMBLY + [pltpu.VMEM((3 * C, 9 * C), F32)],
        compiler_params=params(),
        name="weight_terms",
    )(live, body, *halo, grad)


def backward_kernel(live_ref, body, *refs):
    halo, (weight_ref, mask_ref, out_ref, ext, rows_ref, cols, sums) = refs[:8], refs[8:]
    ids, _ = slots(live_ref)
    assemble(ids, body, halo, ext, rows_ref)
    convolve(weight_ref, ext, cols, sums)

    def step(x, carry):
        rows = pl.ds(pl.multiple_of((x + 2) * C, C), C)
        own = pl.ds(pl.multiple_of(x * C, C), C)
        out_ref[own, :] = (sums[rows, :] * mask_ref[x]).astype(BF16)
        return carry

    lax.fori_loop(0, B, step, 0)


def backward(live, body, halo, weight, mask):
    return pl.pallas_call(
        backward_kernel,
        in_specs=[smem()] + [vmem()] * 11,
        out_specs=vmem(),
        out_shape=jax.ShapeDtypeStruct((B * C, W2), BF16),
        scratch_shapes=ASSEMBLY + [pltpu.VMEM((ROWS, W2), F32)],
        compiler_params=params(),
        name="backward",
    )(live, body, *halo, weight, mask)


def unpack_kernel(live_ref, in_ref, out_ref):
    ids, _ = slots(live_ref)
    group = iota((C, 128), 1) // B
    zero = jnp.zeros((C, 128), BF16)
    inside = [group == ids[s] for s in range(2)]
    for y in range(B):
        h, j = y // 8, y % 8
        moved = []
        for s in range(2):
            k = 2 * s + h
            tile = in_ref[:, k * 128 : (k + 1) * 128]
            moved.append(pltpu.roll(tile, wrap(16 * ids[s] - 16 * j), 1))
        out_ref[0, y] = jnp.where(inside[0], moved[0], jnp.where(inside[1], moved[1], zero))


def unpack(live, packed):
    return pl.pallas_call(
        unpack_kernel,
        grid=(B,),
        in_specs=[smem(), pl.BlockSpec((C, W2), lambda x: (x, 0))],
        out_specs=pl.BlockSpec((1, B, C, 128), lambda x: (x, 0, 0, 0)),
        out_shape=jax.ShapeDtypeStruct((B, B, C, 128), BF16),
        compiler_params=params(),
        name="unpack",
    )(live, packed)


def finish_kernel(sum_ref, small_ref, out_ref):
    root = small_ref[2:3, 0:C]
    for a in range(3):
        for k in range(9):
            start = k * C
            pieces = []
            while start < (k + 1) * C:
                j, off = start // 128, start % 128
                stop = min((k + 1) * C, (j + 1) * 128)
                row = j * 288 + (2 - a) * C
                pieces.append(sum_ref[row : row + C, off : off + stop - start].astype(F32))
                start = stop
            block = pieces[0] if len(pieces) == 1 else jnp.concatenate(pieces, axis=1)
            out_ref[9 * a + k] = block.T * root


def finish(sums, small):
    return pl.pallas_call(
        finish_kernel,
        in_specs=[vmem()] * 2,
        out_specs=vmem(),
        out_shape=jax.ShapeDtypeStruct((27, C, C), F32),
        compiler_params=params(),
        name="finish",
    )(sums, small)


def gather_small(values):
    count = lax.axis_size("gx") * lax.axis_size("gy")
    spread = jnp.broadcast_to(values[None], (count,) + values.shape)
    return lax.all_to_all(spread, AXES, 0, 0, tiled=True)


def sum_large(values):
    count = lax.axis_size("gx") * lax.axis_size("gy")
    parts = values.reshape(count, values.shape[0] // count, 128)
    parts = lax.all_to_all(parts, AXES, 0, 0, tiled=True)
    mine = jnp.sum(parts, axis=0)
    spread = jnp.broadcast_to(mine[None], (count,) + mine.shape)
    return lax.all_to_all(spread, AXES, 0, 0, tiled=True).reshape(values.shape)


def body(features, cotangent, weight, bn_gain, bn_shift, voxel_mask, brick_live):
    gain = jnp.pad(bn_gain, (0, 128 - C))[None]
    shift = jnp.pad(bn_shift, (0, 128 - C))[None]
    cube = weight.reshape(3, 3, 3, C, C)
    weight_rows = jnp.transpose(cube[::-1], (0, 4, 1, 2, 3)).reshape(3 * C, 9 * C)
    weight_back = jnp.transpose(cube[:, ::-1, ::-1], (0, 3, 1, 2, 4)).reshape(3 * C, 9 * C)

    packed, mask, *faces = pack_features(brick_live, features, voxel_mask)
    halo = exchange(faces)
    cot = pack_plain(brick_live, cotangent)
    pre, stats = forward(brick_live, packed, halo, weight_rows, mask)
    stats = gather_small(stats)
    gz, stats2 = slope(stats, pre, cot, mask, gain, shift)
    stats2 = gather_small(stats2)
    grad, small, *grad_faces = pre_grad(brick_live, stats, stats2, pre, gz, mask, gain)
    grad_halo = exchange(grad_faces)
    terms = weight_terms(brick_live, packed, halo, grad)
    sums = sum_large(terms)
    back = backward(brick_live, grad, grad_halo, weight_back, mask)
    input_grad = unpack(brick_live, back)
    weight_grad = finish(sums, small)
    return input_grad, weight_grad, small[0, :C], small[1, :C]


def solution(mesh):
    return jax.shard_map(
        body,
        mesh=mesh,
        in_specs=(
            P("gx", "gy", None, None),
            P("gx", "gy", None, None),
            P(),
            P(),
            P(),
            P("gx", "gy", None),
            P("gx", "gy", None),
        ),
        out_specs=(P("gx", "gy", None, None), P(), P(), P()),
        check_vma=False,
    )
```

```python
import functools

import jax
import jax.numpy as jnp
from jax import lax
from jax.experimental import pallas as pl
from jax.experimental.pallas import tpu as pltpu
from jax.sharding import PartitionSpec as P

B = 16
C = 96
NB = 8
W2 = 512
ROWS = 20 * C
EDGE = C + 16
F32 = jnp.float32
BF16 = jnp.bfloat16
AXES = ("gx", "gy")


def params(mib=56):
    return pltpu.CompilerParams(vmem_limit_bytes=mib * 1024 * 1024)


def vmem():
    return pl.BlockSpec(memory_space=pltpu.VMEM)


def smem():
    return pl.BlockSpec(memory_space=pltpu.SMEM)


def iota(shape, dim):
    return lax.broadcasted_iota(jnp.int32, shape, dim)


def slots(live_ref):
    first = jnp.int32(-1)
    second = jnp.int32(-1)
    for j in reversed(range(NB)):
        on = live_ref[0, 0, j] > 0
        second = jnp.where(on, first, second)
        first = jnp.where(on, jnp.int32(j), first)
    first = jnp.maximum(first, 0)
    spare = jnp.bitwise_and(first + 1, NB - 1)
    return first, jnp.where(second >= 0, second, spare)


def wrap(shift):
    return jnp.bitwise_and(shift + 256, 127)


def lane_parts(shape):
    lane = iota(shape, 1)
    return lane >> 6, (lane >> 4) & 3, lane & 15


def scaled(tile, row):
    return (tile.reshape(C // 16, 16, 128) * row[None]).reshape(C, 128)


def flags(cond):
    return jnp.where(cond, 1.0, 0.0).astype(BF16)


def by_slot(first, second, shape=(16, 128)):
    return jnp.where(lane_parts(shape)[0] == 0, first, second)


def fill_selector(sel_ref, ids):
    row = iota((512, 128), 0)
    slot, group, deep = lane_parts((512, 128))
    start = jnp.where(slot == 0, ids[0], ids[1]) * B
    sel_ref[...] = flags(((row >> 7) == group) & ((row & 127) == start + deep))


def emit_sides(x, tiles, ids, sides):
    xa, xb, ya, yb = sides
    odd_x = lax.axis_index("gx") % 2
    odd_y = lax.axis_index("gy") % 2
    group = lane_parts((C, 128))[1]

    @pl.when(x == 0)
    def _():
        tag = by_slot(ids[0], ids[1]).astype(F32).astype(BF16)
        for face in sides:
            for k in range(4):
                face[C:EDGE, k * 128 : (k + 1) * 128] = tag

    for face, where in ((xa, jnp.where(odd_x == 1, 0, B - 1)), (xb, jnp.where(odd_x == 1, B - 1, 0))):

        @pl.when(x == where)
        def _(face=face):
            for k in range(4):
                face[0:C, k * 128 : (k + 1) * 128] = tiles[k]

    spot = x // 4
    lanes = pl.ds(pl.multiple_of(lax.rem(x, 4) * 128, 128), 128)
    low = pltpu.roll(tiles[0], wrap(16 * spot), 1)
    high = pltpu.roll(tiles[3], wrap(16 * spot - 48), 1)
    for face, flip in ((ya, 1), (yb, 0)):
        moved = jnp.where(odd_y == flip, low, high)
        face[0:C, lanes] = jnp.where(group == spot, moved, face[0:C, lanes])


SIDES = [jax.ShapeDtypeStruct((EDGE, W2), BF16)] * 4


PACE = 4


def paced():
    return pl.BlockSpec((PACE * C, W2), lambda t: (t, 0))


def paced_mask():
    return pl.BlockSpec((PACE, 1, W2), lambda t: (t, 0, 0))


def whole(shape):
    return pl.BlockSpec(shape, lambda *a: (0,) * len(shape))


def pack_features_kernel(live_ref, feat_ref, mask_ref, out_ref, live_out, *refs):
    sides, (sel_ref, lhs_ref) = refs[:4], refs[4:]
    t = pl.program_id(0)
    ids = slots(live_ref)

    @pl.when(t == 0)
    def _():
        fill_selector(sel_ref, ids)

    brick = iota((B, 128), 1) >> 4
    column = jnp.zeros((B, 128), F32)
    for j in range(NB):
        column = jnp.where(brick == j, live_ref[0, 0, j].astype(F32), column)
    for u in range(PACE):
        cells = mask_ref[u].astype(F32) * column
        for y in range(B):
            row = jnp.broadcast_to(cells[y : y + 1, :], (16, 128)).astype(BF16)
            base, lanes = (4 * u + y % 4) * EDGE, slice((y // 4) * 128, (y // 4 + 1) * 128)
            lhs_ref[base : base + C, lanes] = scaled(feat_ref[u, y], row)
            lhs_ref[base + C : base + EDGE, lanes] = row
    moved = jnp.dot(lhs_ref[...], sel_ref[...], preferred_element_type=F32)
    for u in range(PACE):
        tiles = []
        for m in range(4):
            lanes = slice(m * 128, (m + 1) * 128)
            base = (4 * u + m) * EDGE
            tile = moved[base : base + C].astype(BF16)
            out_ref[u * C : (u + 1) * C, lanes] = tile
            live_out[u, :, lanes] = moved[base + C : base + C + 1]
            tiles.append(tile)
        emit_sides(PACE * t + u, tiles, ids, sides)


def pack_features(live, features, mask):
    return pl.pallas_call(
        pack_features_kernel,
        grid=(B // PACE,),
        in_specs=[
            smem(),
            pl.BlockSpec((PACE, B, C, 128), lambda t: (t, 0, 0, 0)),
            pl.BlockSpec((PACE, B, 128), lambda t: (t, 0, 0)),
        ],
        out_specs=[paced(), paced_mask()]
        + [whole(f.shape) for f in SIDES],
        out_shape=[
            jax.ShapeDtypeStruct((B * C, W2), BF16),
            jax.ShapeDtypeStruct((B, 1, W2), F32),
        ]
        + SIDES,
        scratch_shapes=[pltpu.VMEM((512, 128), BF16), pltpu.VMEM((PACE * 4 * EDGE, 512), BF16)],
        compiler_params=params(),
        name="pack_features",
    )(live, features, mask)


def pack_plain_kernel(live_ref, feat_ref, out_ref, sel_ref, lhs_ref):
    ids = slots(live_ref)

    @pl.when(pl.program_id(0) == 0)
    def _():
        fill_selector(sel_ref, ids)

    for u in range(PACE):
        for y in range(B):
            base, lanes = (4 * u + y % 4) * C, slice((y // 4) * 128, (y // 4 + 1) * 128)
            lhs_ref[base : base + C, lanes] = feat_ref[u, y]
    moved = jnp.dot(lhs_ref[...], sel_ref[...], preferred_element_type=F32)
    for u in range(PACE):
        for m in range(4):
            base = (4 * u + m) * C
            out_ref[u * C : (u + 1) * C, m * 128 : (m + 1) * 128] = moved[base : base + C].astype(
                BF16
            )


def pack_plain(live, values):
    return pl.pallas_call(
        pack_plain_kernel,
        grid=(B // PACE,),
        in_specs=[smem(), pl.BlockSpec((PACE, B, C, 128), lambda t: (t, 0, 0, 0))],
        out_specs=paced(),
        out_shape=jax.ShapeDtypeStruct((B * C, W2), BF16),
        scratch_shapes=[pltpu.VMEM((512, 128), BF16), pltpu.VMEM((PACE * 4 * C, 512), BF16)],
        compiler_params=params(),
        name="pack_cotangent",
    )(live, values)


def pick(odd, first, second):
    return jnp.where(odd == 1, first, second), jnp.where(odd == 1, second, first)


def relay_kernel(xa, xb, ya, yb, ya_out, yb_out):
    odd_x = lax.axis_index("gx") % 2
    odd_y = lax.axis_index("gy") % 2
    group = lane_parts((EDGE, 128))[1]
    zero = jnp.zeros((EDGE, 128), BF16)
    edges = []
    for tile, turn in ((0, 0), (3, 80)):
        lanes = slice(tile * 128, (tile + 1) * 128)
        below, above = pick(odd_x, xa[:, lanes], xb[:, lanes])
        if turn:
            below = pltpu.roll(below, turn, 1)
        above = pltpu.roll(above, (turn + 16) % 128, 1)
        edges.append(jnp.where(group == 0, below, jnp.where(group == 1, above, zero)))
    high_first = jnp.where(odd_y == 1, edges[0], edges[1])
    low_first = jnp.where(odd_y == 1, edges[1], edges[0])
    ya_out[:, 0:W2] = ya[...]
    yb_out[:, 0:W2] = yb[...]
    ya_out[:, W2:640] = high_first
    yb_out[:, W2:640] = low_first


def relay(xa, xb, ya, yb):
    return pl.pallas_call(
        relay_kernel,
        in_specs=[vmem()] * 4,
        out_specs=[vmem()] * 2,
        out_shape=[jax.ShapeDtypeStruct((EDGE, 640), BF16)] * 2,
        compiler_params=params(),
        name="relay",
    )(xa, xb, ya, yb)


def swap(values, axis, first):
    count = lax.axis_size(axis)
    pairs = []
    for i in range(count):
        j = i ^ 1 if first else ((i + 1) ^ 1) - 1
        if 0 <= j < count:
            pairs.append((i, j))
    return lax.ppermute(values, axis, pairs)


def exchange(sides, beside):
    xa, xb, ya, yb = sides
    xa = swap(xa, "gx", True)
    xb = swap(xb, "gx", False)
    xa, xb, beside = lax.optimization_barrier((xa, xb, beside))
    ya, yb = relay(xa, xb, ya, yb)
    return (xa, xb, swap(ya, "gy", True), swap(yb, "gy", False)), beside


HALO = [(EDGE, W2), (EDGE, W2), (EDGE, 640), (EDGE, 640)]


class Columns:
    def __init__(self, ids, halo, edge_ref, rows_ref):
        self.halo, self.edge_ref, self.rows_ref = halo, edge_ref, rows_ref
        self.ids = ids
        slot, group, deep = lane_parts((16, 128))
        after = (ids[1] == ids[0] + 1) & (ids[1] > 0)
        near = jnp.where(after, 1, 0)
        self.keep_low = flags(deep > 0)
        self.keep_high = flags(deep < 15)
        self.at_low = flags(deep == 0)
        self.at_high = flags(deep == 15)
        self.from_next = flags((deep == 15) & (slot < near))
        self.from_last = flags((deep == 0) & (slot + near == 2))
        self.first = flags(group == 0)
        self.not_first = flags(group > 0)
        self.last = flags(group == 3)
        self.not_last = flags(group < 3)

    def prepare(self):
        xa, xb, ya, yb = self.halo
        odd_x = lax.axis_index("gx") % 2
        odd_y = lax.axis_index("gy") % 2
        mine = by_slot(self.ids[0], self.ids[1]).astype(F32)

        def shifted(cells):
            tag = cells[C:EDGE].astype(F32)
            turned = pltpu.roll(tag, 64, 1)
            body = cells[0:C]
            other = pltpu.roll(body, 64, 1)
            under, here, over = [
                scaled(body, flags(tag == mine + d)) + scaled(other, flags(turned == mine + d))
                for d in (-1.0, 0.0, 1.0)
            ]
            return (
                scaled(pltpu.roll(here, 1, 1), self.keep_low)
                + scaled(pltpu.roll(under, 113, 1), self.at_low),
                here,
                scaled(pltpu.roll(here, 127, 1), self.keep_high)
                + scaled(pltpu.roll(over, 15, 1), self.at_high),
            )

        def lanes(k):
            return slice(k * 128, (k + 1) * 128)

        for k in range(5):
            for way, cells in enumerate(pick(odd_y, ya[:, lanes(k)], yb[:, lanes(k)])):
                for dz, tile in enumerate(shifted(cells)):
                    self.rows_ref[way, dz, :, lanes(k)] = tile
        for k in range(4):
            for way, cells in enumerate(pick(odd_x, xa[:, lanes(k)], xb[:, lanes(k)])):
                for dz, tile in enumerate(shifted(cells)):
                    self.edge_ref[way, dz, :, lanes(k)] = tile

    def store(self, cols, dz, tiles, below, above):
        head = scaled(pltpu.roll(tiles[3], 16, 1), self.not_first) + scaled(below, self.first)
        tail = scaled(pltpu.roll(tiles[0], 112, 1), self.not_last) + scaled(above, self.last)
        line = [head] + list(tiles) + [tail]
        for dy in range(3):
            k = dy * 3 + dz
            for m in range(4):
                cols[k * C : (k + 1) * C, m * 128 : (m + 1) * 128] = line[dy + m]

    def edge(self, way, cols):
        for dz in range(3):
            tiles = [self.edge_ref[way, dz, :, m * 128 : (m + 1) * 128] for m in range(4)]
            low = self.rows_ref[0, dz, :, W2:640]
            high = self.rows_ref[1, dz, :, W2:640]
            self.store(
                cols,
                dz,
                tiles,
                pltpu.roll(low, 112, 1) if way else low,
                pltpu.roll(high, 32 if way else 48, 1),
            )

    def inner(self, x, body, cols):
        here = [body[:, m * 128 : (m + 1) * 128] for m in range(4)]
        spot = x // 4
        lanes = pl.ds(pl.multiple_of(lax.rem(x, 4) * 128, 128), 128)
        for dz in range(3):
            if dz == 0:
                tiles = [
                    scaled(pltpu.roll(t, 1, 1), self.keep_low)
                    + scaled(pltpu.roll(t, 49, 1), self.from_last)
                    for t in here
                ]
            elif dz == 1:
                tiles = here
            else:
                tiles = [
                    scaled(pltpu.roll(t, 127, 1), self.keep_high)
                    + scaled(pltpu.roll(t, 79, 1), self.from_next)
                    for t in here
                ]
            below = pltpu.roll(self.rows_ref[0, dz, :, lanes], wrap(-16 * spot), 1)
            above = pltpu.roll(self.rows_ref[1, dz, :, lanes], wrap(48 - 16 * spot), 1)
            self.store(cols, dz, tiles, below, above)


ASSEMBLY = [
    pltpu.VMEM((2, 3, C, W2), BF16),
    pltpu.VMEM((2, 3, C, 640), BF16),
    pltpu.VMEM((2, 9 * C, W2), BF16),
]
STEPS = B // 2 + 1


def run_planes(live_ref, body_ref, halo, edge_ref, rows_ref, cols_ref, use):
    t = pl.program_id(0)
    ids = slots(live_ref)
    columns = Columns(ids, halo, edge_ref, rows_ref)
    even, odd = cols_ref.at[0], cols_ref.at[1]

    @pl.when(t == 0)
    def _():
        columns.prepare()
        columns.edge(0, even)

    @pl.when(t < STEPS - 1)
    def _():
        columns.inner(2 * t, body_ref[0:C, :], odd)
        use(2 * t, even)
        columns.inner(2 * t + 1, body_ref[C : 2 * C, :], even)
        use(2 * t + 1, odd)

    @pl.when(t == STEPS - 1)
    def _():
        columns.edge(1, odd)
        use(2 * t, even)
        use(2 * t + 1, odd)


def plane_block():
    return pl.BlockSpec((2 * C, W2), lambda t: (jnp.minimum(t, B // 2 - 1), 0))


def late_block():
    return pl.BlockSpec((2 * C, W2), lambda t: (jnp.maximum(t - 1, 0), 0))


def fold(values):
    return (values[:, 0:128] + values[:, 128:256]) + (values[:, 256:384] + values[:, 384:512])


def to_row(column_tile):
    column = jnp.sum(column_tile, axis=1, keepdims=True)
    diag = iota((C, 128), 0) == iota((C, 128), 1)
    return jnp.sum(jnp.where(diag, column, 0.0), axis=0, keepdims=True)


def to_column(row):
    diag = iota((C, 128), 0) == iota((C, 128), 1)
    return jnp.sum(jnp.where(diag, row, 0.0), axis=1, keepdims=True)


def add_product(weight_ref, sums):
    def use(i, cols):
        part = jnp.dot(weight_ref[...], cols[...], preferred_element_type=F32)
        rows = pl.ds(pl.multiple_of(i * C, C), 3 * C)
        sums[rows, :] += part

    return use


def forward_kernel(live_ref, body_ref, *refs):
    halo, (weight_ref, mask_ref, pre_ref, stat_ref) = refs[:4], refs[4:8]
    edge_ref, rows_ref, cols_ref, sums, acc = refs[8:]
    t = pl.program_id(0)

    @pl.when(t == 0)
    def _():
        sums[...] = jnp.zeros_like(sums)
        acc[...] = jnp.zeros_like(acc)

    run_planes(
        live_ref, body_ref, halo, edge_ref, rows_ref, cols_ref, add_product(weight_ref, sums)
    )

    @pl.when(t > 0)
    def _():
        for u in range(2):
            values = sums[pl.ds(pl.multiple_of((2 * t + u) * C, C), C), :]
            mask = mask_ref[2 * t - 2 + u]
            held = values * mask
            pre_ref[u * C : (u + 1) * C, :] = values
            acc[0] += fold(held)
            acc[1] += fold(held * values)
            acc[2, 0:1, :] += fold(mask)

    @pl.when(t == STEPS - 1)
    def _():
        stat_ref[...] = jnp.zeros_like(stat_ref)
        stat_ref[0:1, :] = to_row(acc[0])
        stat_ref[1:2, :] = to_row(acc[1])
        stat_ref[2:3, :] = jnp.full((1, 128), 1.0, F32) * jnp.sum(acc[2, 0:1, :])


def forward(live, body, halo, weight, mask):
    return pl.pallas_call(
        forward_kernel,
        grid=(STEPS,),
        in_specs=[smem(), plane_block()]
        + [whole(h) for h in HALO]
        + [whole(weight.shape), whole(mask.shape)],
        out_specs=[late_block(), whole((8, 128))],
        out_shape=[
            jax.ShapeDtypeStruct((B * C, W2), F32),
            jax.ShapeDtypeStruct((8, 128), F32),
        ],
        scratch_shapes=ASSEMBLY + [pltpu.VMEM((ROWS, W2), F32), pltpu.VMEM((3, C, 128), F32)],
        compiler_params=params(),
        name="forward",
    )(live, body, *halo, weight, mask)


def moments(stat_ref):
    total = jnp.sum(stat_ref[...], axis=0)
    voxels = total[2:3, :]
    mean = total[0:1, :] / voxels
    var = total[1:2, :] / voxels - mean * mean
    return voxels, mean, lax.rsqrt(var + 1e-05)


def slope_kernel(
    stat_ref, pre_ref, cot_ref, mask_ref, gain_ref, shift_ref, gz_ref, out_ref, col_ref, acc
):
    t = pl.program_id(0)

    @pl.when(t == 0)
    def _():
        voxels, mean, inv = moments(stat_ref)
        for k, row in enumerate((mean, inv, gain_ref[...], shift_ref[...])):
            col_ref[k] = jnp.broadcast_to(to_column(row), (C, 128))
        acc[...] = jnp.zeros_like(acc)

    mean, inv, gain, shift = [col_ref[k] for k in range(4)]
    total = acc[0]
    cross = acc[1]
    for u in range(PACE):
        rows = slice(u * C, (u + 1) * C)
        for k in range(4):
            lanes = slice(k * 128, (k + 1) * 128)
            normed = (pre_ref[rows, lanes] - mean) * inv
            zed = gain * normed + shift
            sig = 0.5 + 0.5 * jnp.tanh(0.5 * zed)
            gz = (
                mask_ref[u][:, lanes]
                * cot_ref[rows, lanes].astype(F32)
                * (sig * (1.0 + zed * (1.0 - sig)))
            )
            gz_ref[rows, lanes] = gz
            total += gz
            cross += gz * normed
    acc[0] = total
    acc[1] = cross

    @pl.when(t == B // PACE - 1)
    def _():
        out_ref[...] = jnp.zeros_like(out_ref)
        out_ref[0:1, :] = to_row(acc[0])
        out_ref[1:2, :] = to_row(acc[1])


def slope(stats, pre, cot, mask, gain, shift):
    return pl.pallas_call(
        slope_kernel,
        grid=(B // PACE,),
        in_specs=[
            whole(stats.shape),
            paced(),
            paced(),
            paced_mask(),
            whole((1, 128)),
            whole((1, 128)),
        ],
        out_specs=[paced(), whole((8, 128))],
        out_shape=[
            jax.ShapeDtypeStruct((B * C, W2), F32),
            jax.ShapeDtypeStruct((8, 128), F32),
        ],
        scratch_shapes=[pltpu.VMEM((4, C, 128), F32), pltpu.VMEM((2, C, 128), F32)],
        compiler_params=params(),
        name="slope",
    )(stats, pre, cot, mask, gain, shift)


def pre_grad_kernel(
    live_ref, stat_ref, stat2_ref, pre_ref, gz_ref, mask_ref, gain_ref, out_ref, small_ref, *refs
):
    sides, (col_ref,) = refs[:4], refs[4:]
    t = pl.program_id(0)
    ids = slots(live_ref)

    @pl.when(t == 0)
    def _():
        voxels, mean, inv = moments(stat_ref)
        total = jnp.sum(stat2_ref[...], axis=0)
        root = 1.0 / jnp.sqrt(voxels)
        small_ref[...] = jnp.zeros_like(small_ref)
        small_ref[0:1, :] = total[1:2, :] * root
        small_ref[1:2, :] = total[0:1, :] * root
        small_ref[2:3, :] = root
        rows = (mean, inv, gain_ref[...] * inv, total[0:1, :] / voxels, total[1:2, :] / voxels)
        for k, row in enumerate(rows):
            col_ref[k] = jnp.broadcast_to(to_column(row), (C, 128))

    mean, inv, scale, first, second = [col_ref[k] for k in range(5)]
    for u in range(PACE):
        rows = slice(u * C, (u + 1) * C)
        tiles = []
        for k in range(4):
            lanes = slice(k * 128, (k + 1) * 128)
            normed = (pre_ref[rows, lanes] - mean) * inv
            tile = (
                mask_ref[u][:, lanes] * scale * (gz_ref[rows, lanes] - first - normed * second)
            ).astype(BF16)
            out_ref[rows, lanes] = tile
            tiles.append(tile)
        emit_sides(PACE * t + u, tiles, ids, sides)


def pre_grad(live, stats, stats2, pre, gz, mask, gain):
    return pl.pallas_call(
        pre_grad_kernel,
        grid=(B // PACE,),
        in_specs=[
            smem(),
            whole(stats.shape),
            whole(stats2.shape),
            paced(),
            paced(),
            paced_mask(),
            whole((1, 128)),
        ],
        out_specs=[paced(), whole((8, 128))] + [whole(f.shape) for f in SIDES],
        out_shape=[
            jax.ShapeDtypeStruct((B * C, W2), BF16),
            jax.ShapeDtypeStruct((8, 128), F32),
        ]
        + SIDES,
        scratch_shapes=[pltpu.VMEM((5, C, 128), F32)],
        compiler_params=params(),
        name="pre_grad",
    )(live, stats, stats2, pre, gz, mask, gain)


def weight_kernel(live_ref, body_ref, *refs):
    halo, (grad_ref, out_ref) = refs[:4], refs[4:6]
    edge_ref, rows_ref, cols_ref, padded, total = refs[6:]
    t = pl.program_id(0)

    @pl.when(t == 0)
    def _():
        padded[0 : 2 * C, :] = jnp.zeros((2 * C, W2), BF16)
        padded[2 * C : 18 * C, :] = grad_ref[...]
        padded[18 * C : ROWS, :] = jnp.zeros((2 * C, W2), BF16)
        total[...] = jnp.zeros_like(total)

    def use(i, cols):
        rows = pl.ds(pl.multiple_of(i * C, C), 3 * C)
        total[...] += lax.dot_general(
            padded[rows, :], cols[...], (((1,), (1,)), ((), ())), preferred_element_type=F32
        )

    run_planes(live_ref, body_ref, halo, edge_ref, rows_ref, cols_ref, use)

    @pl.when(t == STEPS - 1)
    def _():
        for j in range(6):
            out_ref[j * 288 : (j + 1) * 288, :] = total[:, j * 128 : (j + 1) * 128]
        out_ref[6 * 288 : 2048, :] = jnp.zeros((2048 - 6 * 288, 128), F32)
        out_ref[6 * 288 : 7 * 288, 0:96] = total[:, 768:864]


def weight_terms(live, body, halo, grad):
    return pl.pallas_call(
        weight_kernel,
        grid=(STEPS,),
        in_specs=[smem(), plane_block()] + [whole(h) for h in HALO] + [whole(grad.shape)],
        out_specs=whole((2048, 128)),
        out_shape=jax.ShapeDtypeStruct((2048, 128), F32),
        scratch_shapes=ASSEMBLY
        + [pltpu.VMEM((ROWS, W2), BF16), pltpu.VMEM((3 * C, 9 * C), F32)],
        compiler_params=params(),
        name="weight_terms",
    )(live, body, *halo, grad)


def backward_kernel(live_ref, body_ref, *refs):
    halo, (weight_ref, mask_ref, out_ref) = refs[:4], refs[4:7]
    edge_ref, rows_ref, cols_ref, sums, spread = refs[7:]
    t = pl.program_id(0)

    @pl.when(t == 0)
    def _():
        sums[...] = jnp.zeros_like(sums)
        ids = slots(live_ref)
        row, lane = iota((128, W2), 0), iota((128, W2), 1)
        start = jnp.where((row >> 6) == 0, ids[0], ids[1]) * B
        spread[...] = flags(
            (((row >> 4) & 3) == (lane >> 7)) & ((lane & 127) == start + (row & 15))
        )

    run_planes(
        live_ref, body_ref, halo, edge_ref, rows_ref, cols_ref, add_product(weight_ref, sums)
    )

    @pl.when(t > 0)
    def _():
        for u in range(2):
            rows = pl.ds(pl.multiple_of((2 * t + u) * C, C), C)
            mask = mask_ref[2 * t - 2 + u]
            for m in range(4):
                lanes = slice(m * 128, (m + 1) * 128)
                tile = (sums[rows, lanes] * mask[:, lanes]).astype(BF16)
                moved = jnp.dot(tile, spread[...], preferred_element_type=F32)
                for g in range(4):
                    out_ref[u, 4 * g + m] = moved[:, g * 128 : (g + 1) * 128].astype(BF16)


def backward(live, body, halo, weight, mask):
    return pl.pallas_call(
        backward_kernel,
        grid=(STEPS,),
        in_specs=[smem(), plane_block()]
        + [whole(h) for h in HALO]
        + [whole(weight.shape), whole(mask.shape)],
        out_specs=pl.BlockSpec((2, B, C, 128), lambda t: (jnp.maximum(t - 1, 0), 0, 0, 0)),
        out_shape=jax.ShapeDtypeStruct((B, B, C, 128), BF16),
        scratch_shapes=ASSEMBLY + [pltpu.VMEM((ROWS, W2), F32), pltpu.VMEM((128, W2), BF16)],
        compiler_params=params(),
        name="backward",
    )(live, body, *halo, weight, mask)


def finish_kernel(sum_ref, small_ref, out_ref):
    root = small_ref[2:3, 0:C]
    for a in range(3):
        for k in range(9):
            start = k * C
            pieces = []
            while start < (k + 1) * C:
                j, off = start // 128, start % 128
                stop = min((k + 1) * C, (j + 1) * 128)
                row = j * 288 + (2 - a) * C
                pieces.append(sum_ref[row : row + C, off : off + stop - start].astype(F32))
                start = stop
            block = pieces[0] if len(pieces) == 1 else jnp.concatenate(pieces, axis=1)
            out_ref[9 * a + k] = block.T * root


def finish(sums, small):
    return pl.pallas_call(
        finish_kernel,
        in_specs=[vmem()] * 2,
        out_specs=vmem(),
        out_shape=jax.ShapeDtypeStruct((27, C, C), F32),
        compiler_params=params(),
        name="finish",
    )(sums, small)


def arrange_kernel(weight_ref, fwd_ref, back_ref):
    for a in range(3):
        for k in range(9):
            block = weight_ref[9 * a + k]
            fwd_ref[(2 - a) * C : (3 - a) * C, k * C : (k + 1) * C] = block.T
            back_ref[a * C : (a + 1) * C, (8 - k) * C : (9 - k) * C] = block


def arrange(weight):
    return pl.pallas_call(
        arrange_kernel,
        in_specs=[vmem()],
        out_specs=[vmem()] * 2,
        out_shape=[jax.ShapeDtypeStruct((3 * C, 9 * C), BF16)] * 2,
        compiler_params=params(),
        name="arrange",
    )(weight)


def gather_small(values):
    count = lax.axis_size("gx") * lax.axis_size("gy")
    spread = jnp.broadcast_to(values[None], (count,) + values.shape)
    return lax.all_to_all(spread, AXES, 0, 0, tiled=True)


def scatter_large(values):
    count = lax.axis_size("gx") * lax.axis_size("gy")
    parts = values.reshape(count, values.shape[0] // count, 128)
    return lax.all_to_all(parts, AXES, 0, 0, tiled=True)


def gather_large(parts):
    mine = jnp.sum(parts, axis=0)
    spread = jnp.broadcast_to(mine[None], parts.shape)
    return lax.all_to_all(spread, AXES, 0, 0, tiled=True).reshape(-1, 128)


def body(features, cotangent, weight, bn_gain, bn_shift, voxel_mask, brick_live):
    gain = jnp.pad(bn_gain, (0, 128 - C))[None]
    shift = jnp.pad(bn_shift, (0, 128 - C))[None]
    packed, mask, *sides = pack_features(brick_live, features, voxel_mask)
    weight_rows, weight_back = arrange(weight)
    halo, (weight_rows, weight_back) = exchange(sides, (weight_rows, weight_back))
    pre, stats = forward(brick_live, packed, halo, weight_rows, mask)
    cotangent, stats = lax.optimization_barrier((cotangent, stats))
    stats = gather_small(stats)
    cot = pack_plain(brick_live, cotangent)
    gz, stats2 = slope(stats, pre, cot, mask, gain, shift)
    stats2 = gather_small(stats2)
    grad, small, *grad_sides = pre_grad(brick_live, stats, stats2, pre, gz, mask, gain)
    terms = weight_terms(brick_live, packed, halo, grad)
    grad_halo, terms = exchange(grad_sides, terms)
    parts = scatter_large(terms)
    parts, grad_halo = lax.optimization_barrier((parts, grad_halo))
    sums = gather_large(parts)
    input_grad = backward(brick_live, grad, grad_halo, weight_back, mask)
    weight_grad = finish(sums, small)
    return input_grad, weight_grad, small[0, :C], small[1, :C]


def solution(mesh):
    return jax.shard_map(
        body,
        mesh=mesh,
        in_specs=(
            P("gx", "gy", None, None),
            P("gx", "gy", None, None),
            P(),
            P(),
            P(),
            P("gx", "gy", None),
            P("gx", "gy", None),
        ),
        out_specs=(P("gx", "gy", None, None), P(), P(), P()),
        check_vma=False,
    )
```

```python
import functools

import jax
import jax.numpy as jnp
from jax import lax
from jax.experimental import pallas as pl
from jax.experimental.pallas import tpu as pltpu
from jax.sharding import PartitionSpec as P

B = 16
C = 96
NB = 8
W2 = 512
ROWS = 20 * C
EDGE = C + 16
F32 = jnp.float32
BF16 = jnp.bfloat16
AXES = ("gx", "gy")


def params(mib=56):
    return pltpu.CompilerParams(vmem_limit_bytes=mib * 1024 * 1024)


def vmem():
    return pl.BlockSpec(memory_space=pltpu.VMEM)


def smem():
    return pl.BlockSpec(memory_space=pltpu.SMEM)


def iota(shape, dim):
    return lax.broadcasted_iota(jnp.int32, shape, dim)


def slots(live_ref):
    first = jnp.int32(-1)
    second = jnp.int32(-1)
    for j in reversed(range(NB)):
        on = live_ref[0, 0, j] > 0
        second = jnp.where(on, first, second)
        first = jnp.where(on, jnp.int32(j), first)
    first = jnp.maximum(first, 0)
    spare = jnp.bitwise_and(first + 1, NB - 1)
    return first, jnp.where(second >= 0, second, spare)


def wrap(shift):
    return jnp.bitwise_and(shift + 256, 127)


def lane_parts(shape):
    lane = iota(shape, 1)
    return lane >> 6, (lane >> 4) & 3, lane & 15


def scaled(tile, row):
    return (tile.reshape(C // 16, 16, 128) * row[None]).reshape(C, 128)


def flags(cond):
    return jnp.where(cond, 1.0, 0.0).astype(BF16)


def by_slot(first, second, shape=(16, 128)):
    return jnp.where(lane_parts(shape)[0] == 0, first, second)


def fill_selector(sel_ref, ids):
    row = iota((512, 128), 0)
    slot, group, deep = lane_parts((512, 128))
    start = jnp.where(slot == 0, ids[0], ids[1]) * B
    sel_ref[...] = flags(((row >> 7) == group) & ((row & 127) == start + deep))


def emit_sides(x, tiles, ids, sides):
    xa, xb, ya, yb = sides
    odd_x = lax.axis_index("gx") % 2
    odd_y = lax.axis_index("gy") % 2
    group = lane_parts((C, 128))[1]

    @pl.when(x == 0)
    def _():
        tag = by_slot(ids[0], ids[1]).astype(F32).astype(BF16)
        for face in sides:
            for k in range(4):
                face[C:EDGE, k * 128 : (k + 1) * 128] = tag

    for face, where in ((xa, jnp.where(odd_x == 1, 0, B - 1)), (xb, jnp.where(odd_x == 1, B - 1, 0))):

        @pl.when(x == where)
        def _(face=face):
            for k in range(4):
                face[0:C, k * 128 : (k + 1) * 128] = tiles[k]

    spot = x // 4
    lanes = pl.ds(pl.multiple_of(lax.rem(x, 4) * 128, 128), 128)
    low = pltpu.roll(tiles[0], wrap(16 * spot), 1)
    high = pltpu.roll(tiles[3], wrap(16 * spot - 48), 1)
    for face, flip in ((ya, 1), (yb, 0)):
        moved = jnp.where(odd_y == flip, low, high)
        face[0:C, lanes] = jnp.where(group == spot, moved, face[0:C, lanes])


SIDES = [jax.ShapeDtypeStruct((EDGE, W2), BF16)] * 4


PACE = 8


def paced():
    return pl.BlockSpec((PACE * C, W2), lambda t: (t, 0))


def paced_mask():
    return pl.BlockSpec((PACE, 1, W2), lambda t: (t, 0, 0))


def whole(shape):
    return pl.BlockSpec(shape, lambda *a: (0,) * len(shape))


def pack_features_kernel(live_ref, feat_ref, mask_ref, out_ref, live_out, *refs):
    sides, (sel_ref, lhs_ref) = refs[:4], refs[4:]
    t = pl.program_id(0)
    ids = slots(live_ref)

    @pl.when(t == 0)
    def _():
        fill_selector(sel_ref, ids)

    brick = iota((B, 128), 1) >> 4
    column = jnp.zeros((B, 128), F32)
    for j in range(NB):
        column = jnp.where(brick == j, live_ref[0, 0, j].astype(F32), column)
    for u in range(PACE):
        cells = mask_ref[u].astype(F32) * column
        for y in range(B):
            row = jnp.broadcast_to(cells[y : y + 1, :], (16, 128)).astype(BF16)
            base, lanes = (4 * u + y % 4) * EDGE, slice((y // 4) * 128, (y // 4 + 1) * 128)
            lhs_ref[base : base + C, lanes] = scaled(feat_ref[u, y], row)
            lhs_ref[base + C : base + EDGE, lanes] = row
    moved = jnp.dot(lhs_ref[...], sel_ref[...], preferred_element_type=F32)
    for u in range(PACE):
        tiles = []
        for m in range(4):
            lanes = slice(m * 128, (m + 1) * 128)
            base = (4 * u + m) * EDGE
            tile = moved[base : base + C].astype(BF16)
            out_ref[u * C : (u + 1) * C, lanes] = tile
            live_out[u, :, lanes] = moved[base + C : base + C + 1]
            tiles.append(tile)
        emit_sides(PACE * t + u, tiles, ids, sides)


def pack_features(live, features, mask):
    return pl.pallas_call(
        pack_features_kernel,
        grid=(B // PACE,),
        in_specs=[
            smem(),
            pl.BlockSpec((PACE, B, C, 128), lambda t: (t, 0, 0, 0)),
            pl.BlockSpec((PACE, B, 128), lambda t: (t, 0, 0)),
        ],
        out_specs=[paced(), paced_mask()]
        + [whole(f.shape) for f in SIDES],
        out_shape=[
            jax.ShapeDtypeStruct((B * C, W2), BF16),
            jax.ShapeDtypeStruct((B, 1, W2), F32),
        ]
        + SIDES,
        scratch_shapes=[pltpu.VMEM((512, 128), BF16), pltpu.VMEM((PACE * 4 * EDGE, 512), BF16)],
        compiler_params=params(),
        name="pack_features",
    )(live, features, mask)


def pack_plain_kernel(live_ref, feat_ref, out_ref, sel_ref, lhs_ref):
    ids = slots(live_ref)

    @pl.when(pl.program_id(0) == 0)
    def _():
        fill_selector(sel_ref, ids)

    for u in range(PACE):
        for y in range(B):
            base, lanes = (4 * u + y % 4) * C, slice((y // 4) * 128, (y // 4 + 1) * 128)
            lhs_ref[base : base + C, lanes] = feat_ref[u, y]
    moved = jnp.dot(lhs_ref[...], sel_ref[...], preferred_element_type=F32)
    for u in range(PACE):
        for m in range(4):
            base = (4 * u + m) * C
            out_ref[u * C : (u + 1) * C, m * 128 : (m + 1) * 128] = moved[base : base + C].astype(
                BF16
            )


def pack_plain(live, values):
    return pl.pallas_call(
        pack_plain_kernel,
        grid=(B // PACE,),
        in_specs=[smem(), pl.BlockSpec((PACE, B, C, 128), lambda t: (t, 0, 0, 0))],
        out_specs=paced(),
        out_shape=jax.ShapeDtypeStruct((B * C, W2), BF16),
        scratch_shapes=[pltpu.VMEM((512, 128), BF16), pltpu.VMEM((PACE * 4 * C, 512), BF16)],
        compiler_params=params(),
        name="pack_cotangent",
    )(live, values)


def pick(odd, first, second):
    return jnp.where(odd == 1, first, second), jnp.where(odd == 1, second, first)


def relay_kernel(xa, xb, ya, yb, ya_out, yb_out):
    odd_x = lax.axis_index("gx") % 2
    odd_y = lax.axis_index("gy") % 2
    group = lane_parts((EDGE, 128))[1]
    zero = jnp.zeros((EDGE, 128), BF16)
    edges = []
    for tile, turn in ((0, 0), (3, 80)):
        lanes = slice(tile * 128, (tile + 1) * 128)
        below, above = pick(odd_x, xa[:, lanes], xb[:, lanes])
        if turn:
            below = pltpu.roll(below, turn, 1)
        above = pltpu.roll(above, (turn + 16) % 128, 1)
        edges.append(jnp.where(group == 0, below, jnp.where(group == 1, above, zero)))
    high_first = jnp.where(odd_y == 1, edges[0], edges[1])
    low_first = jnp.where(odd_y == 1, edges[1], edges[0])
    ya_out[:, 0:W2] = ya[...]
    yb_out[:, 0:W2] = yb[...]
    ya_out[:, W2:640] = high_first
    yb_out[:, W2:640] = low_first


def relay(xa, xb, ya, yb):
    return pl.pallas_call(
        relay_kernel,
        in_specs=[vmem()] * 4,
        out_specs=[vmem()] * 2,
        out_shape=[jax.ShapeDtypeStruct((EDGE, 640), BF16)] * 2,
        compiler_params=params(),
        name="relay",
    )(xa, xb, ya, yb)


def swap(values, axis, first):
    count = lax.axis_size(axis)
    pairs = []
    for i in range(count):
        j = i ^ 1 if first else ((i + 1) ^ 1) - 1
        if 0 <= j < count:
            pairs.append((i, j))
    return lax.ppermute(values, axis, pairs)


def exchange(sides, beside):
    xa, xb, ya, yb = sides
    xa = swap(xa, "gx", True)
    xb = swap(xb, "gx", False)
    xa, xb, beside = lax.optimization_barrier((xa, xb, beside))
    ya, yb = relay(xa, xb, ya, yb)
    return (xa, xb, swap(ya, "gy", True), swap(yb, "gy", False)), beside


HALO = [(EDGE, W2), (EDGE, W2), (EDGE, 640), (EDGE, 640)]


class Columns:
    def __init__(self, ids, halo, edge_ref, rows_ref):
        self.halo, self.edge_ref, self.rows_ref = halo, edge_ref, rows_ref
        self.ids = ids
        slot, group, deep = lane_parts((16, 128))
        after = (ids[1] == ids[0] + 1) & (ids[1] > 0)
        near = jnp.where(after, 1, 0)
        self.keep_low = flags(deep > 0)
        self.keep_high = flags(deep < 15)
        self.at_low = flags(deep == 0)
        self.at_high = flags(deep == 15)
        self.from_next = flags((deep == 15) & (slot < near))
        self.from_last = flags((deep == 0) & (slot + near == 2))
        self.first = flags(group == 0)
        self.not_first = flags(group > 0)
        self.last = flags(group == 3)
        self.not_last = flags(group < 3)

    def prepare(self):
        xa, xb, ya, yb = self.halo
        odd_x = lax.axis_index("gx") % 2
        odd_y = lax.axis_index("gy") % 2
        mine = by_slot(self.ids[0], self.ids[1]).astype(F32)

        def shifted(cells):
            tag = cells[C:EDGE].astype(F32)
            turned = pltpu.roll(tag, 64, 1)
            body = cells[0:C]
            other = pltpu.roll(body, 64, 1)
            under, here, over = [
                scaled(body, flags(tag == mine + d)) + scaled(other, flags(turned == mine + d))
                for d in (-1.0, 0.0, 1.0)
            ]
            return (
                scaled(pltpu.roll(here, 1, 1), self.keep_low)
                + scaled(pltpu.roll(under, 113, 1), self.at_low),
                here,
                scaled(pltpu.roll(here, 127, 1), self.keep_high)
                + scaled(pltpu.roll(over, 15, 1), self.at_high),
            )

        def lanes(k):
            return slice(k * 128, (k + 1) * 128)

        for k in range(5):
            for way, cells in enumerate(pick(odd_y, ya[:, lanes(k)], yb[:, lanes(k)])):
                for dz, tile in enumerate(shifted(cells)):
                    self.rows_ref[way, dz, :, lanes(k)] = tile
        for k in range(4):
            for way, cells in enumerate(pick(odd_x, xa[:, lanes(k)], xb[:, lanes(k)])):
                for dz, tile in enumerate(shifted(cells)):
                    self.edge_ref[way, dz, :, lanes(k)] = tile

    def store(self, cols, dz, tiles, below, above):
        head = scaled(pltpu.roll(tiles[3], 16, 1), self.not_first) + scaled(below, self.first)
        tail = scaled(pltpu.roll(tiles[0], 112, 1), self.not_last) + scaled(above, self.last)
        line = [head] + list(tiles) + [tail]
        for dy in range(3):
            k = dy * 3 + dz
            for m in range(4):
                cols[k * C : (k + 1) * C, m * 128 : (m + 1) * 128] = line[dy + m]

    def edge(self, way, cols):
        for dz in range(3):
            tiles = [self.edge_ref[way, dz, :, m * 128 : (m + 1) * 128] for m in range(4)]
            low = self.rows_ref[0, dz, :, W2:640]
            high = self.rows_ref[1, dz, :, W2:640]
            self.store(
                cols,
                dz,
                tiles,
                pltpu.roll(low, 112, 1) if way else low,
                pltpu.roll(high, 32 if way else 48, 1),
            )

    def inner(self, x, body, cols):
        here = [body[:, m * 128 : (m + 1) * 128] for m in range(4)]
        spot = x // 4
        lanes = pl.ds(pl.multiple_of(lax.rem(x, 4) * 128, 128), 128)
        for dz in range(3):
            if dz == 0:
                tiles = [
                    scaled(pltpu.roll(t, 1, 1), self.keep_low)
                    + scaled(pltpu.roll(t, 49, 1), self.from_last)
                    for t in here
                ]
            elif dz == 1:
                tiles = here
            else:
                tiles = [
                    scaled(pltpu.roll(t, 127, 1), self.keep_high)
                    + scaled(pltpu.roll(t, 79, 1), self.from_next)
                    for t in here
                ]
            below = pltpu.roll(self.rows_ref[0, dz, :, lanes], wrap(-16 * spot), 1)
            above = pltpu.roll(self.rows_ref[1, dz, :, lanes], wrap(48 - 16 * spot), 1)
            self.store(cols, dz, tiles, below, above)


ASSEMBLY = [
    pltpu.VMEM((2, 3, C, W2), BF16),
    pltpu.VMEM((2, 3, C, 640), BF16),
    pltpu.VMEM((2, 9 * C, W2), BF16),
]


def run_planes(live_ref, body_ref, halo, edge_ref, rows_ref, cols_ref, use):
    t = pl.program_id(0)
    columns = Columns(slots(live_ref), halo, edge_ref, rows_ref)
    bufs = [cols_ref.at[k] for k in range(2)]

    def build(i, buf):
        if isinstance(i, int) and i in (0, 17):
            columns.edge(i // 17, buf)
        else:
            rows = (i - 1) * C
            if not isinstance(i, int):
                rows = pl.multiple_of(rows, C)
            columns.inner(i - 1, body_ref[pl.ds(rows, C), :], buf)

    def pass_over(base, count):
        for j in range(count):
            if not isinstance(base, int) or base + j < 17:
                build(base + j + 1, bufs[(j + 1) % 2])
            use(base + j, bufs[j % 2])

    @pl.when(t == 0)
    def _():
        columns.prepare()
        build(0, bufs[0])
        pass_over(0, 6)

    @pl.when((t > 0) & (t < 3))
    def _():
        pass_over(2 + 4 * t, 4)

    @pl.when(t == 3)
    def _():
        pass_over(14, 4)


def four_planes():
    return pl.BlockSpec((4 * C, W2), lambda t: (t, 0))


def fold(values):
    return (values[:, 0:128] + values[:, 128:256]) + (values[:, 256:384] + values[:, 384:512])


def to_row(column_tile):
    column = jnp.sum(column_tile, axis=1, keepdims=True)
    diag = iota((C, 128), 0) == iota((C, 128), 1)
    return jnp.sum(jnp.where(diag, column, 0.0), axis=0, keepdims=True)


def to_column(row):
    diag = iota((C, 128), 0) == iota((C, 128), 1)
    return jnp.sum(jnp.where(diag, row, 0.0), axis=1, keepdims=True)


def add_product(weight_ref, sums):
    def use(i, cols):
        part = jnp.dot(weight_ref[...], cols[...], preferred_element_type=F32)
        rows = i * C if isinstance(i, int) else pl.multiple_of(i * C, C)
        sums[pl.ds(rows, 2 * C), :] += part[0 : 2 * C]
        sums[pl.ds(rows + 2 * C, C), :] = part[2 * C : 3 * C]

    return use


def forward_kernel(live_ref, body_ref, *refs):
    halo, (weight_ref, mask_ref, pre_ref, stat_ref) = refs[:4], refs[4:8]
    edge_ref, rows_ref, cols_ref, sums, acc = refs[8:]
    t = pl.program_id(0)

    @pl.when(t == 0)
    def _():
        acc[...] = jnp.zeros_like(acc)

    run_planes(
        live_ref, body_ref, halo, edge_ref, rows_ref, cols_ref, add_product(weight_ref, sums)
    )
    for u in range(4):
        values = sums[pl.ds(pl.multiple_of((4 * t + 2 + u) * C, C), C), :]
        mask = mask_ref[4 * t + u]
        held = values * mask
        pre_ref[u * C : (u + 1) * C, :] = values
        acc[0] += fold(held)
        acc[1] += fold(held * values)
        acc[2, 0:1, :] += fold(mask)

    @pl.when(t == 3)
    def _():
        lane = iota((1, 128), 1)
        total = jnp.where(lane == C, jnp.sum(acc[2, 0:1, :]), to_row(acc[0]))
        rows = jnp.concatenate([total, to_row(acc[1])], axis=0)
        stat_ref[...] = jnp.broadcast_to(rows[None], stat_ref.shape)


def devices():
    return lax.axis_size("gx") * lax.axis_size("gy")


def forward(live, body, halo, weight, mask):
    spread = (devices(), 2, 128)
    return pl.pallas_call(
        forward_kernel,
        grid=(4,),
        in_specs=[smem(), whole(body.shape)]
        + [whole(h) for h in HALO]
        + [whole(weight.shape), whole(mask.shape)],
        out_specs=[four_planes(), whole(spread)],
        out_shape=[
            jax.ShapeDtypeStruct((B * C, W2), F32),
            jax.ShapeDtypeStruct(spread, F32),
        ],
        scratch_shapes=ASSEMBLY + [pltpu.VMEM((ROWS, W2), F32), pltpu.VMEM((3, C, 128), F32)],
        compiler_params=params(),
        name="forward",
    )(live, body, *halo, weight, mask)


def moments(stat_ref):
    total = jnp.sum(stat_ref[...], axis=0)
    lane = iota((1, 128), 1)
    voxels = jnp.sum(jnp.where(lane == C, total[0:1, :], 0.0), axis=1, keepdims=True)
    voxels = jnp.broadcast_to(voxels, (1, 128))
    mean = total[0:1, :] / voxels
    var = total[1:2, :] / voxels - mean * mean
    return voxels, mean, lax.rsqrt(var + 1e-05)


def slope_tile(refs, u, k, terms):
    pre_ref, cot_ref, mask_ref = refs
    mean, inv, gain, shift = terms
    rows, lanes = slice(u * C, (u + 1) * C), slice(k * 128, (k + 1) * 128)
    normed = (pre_ref[rows, lanes] - mean) * inv
    zed = gain * normed + shift
    sig = 0.5 + 0.5 * jnp.tanh(0.5 * zed)
    held = mask_ref[u][:, lanes] * cot_ref[rows, lanes].astype(F32)
    return normed, held * (sig * (1.0 + zed * (1.0 - sig)))


def slope_kernel(
    stat_ref, pre_ref, cot_ref, mask_ref, gain_ref, shift_ref, out_ref, col_ref, acc
):
    t = pl.program_id(0)

    @pl.when(t == 0)
    def _():
        voxels, mean, inv = moments(stat_ref)
        for k, row in enumerate((mean, inv, gain_ref[...], shift_ref[...])):
            col_ref[k] = jnp.broadcast_to(to_column(row), (C, 128))
        acc[...] = jnp.zeros_like(acc)

    terms = [col_ref[k] for k in range(4)]
    total = acc[0]
    cross = acc[1]
    for u in range(PACE):
        for k in range(4):
            normed, gz = slope_tile((pre_ref, cot_ref, mask_ref), u, k, terms)
            total += gz
            cross += gz * normed
    acc[0] = total
    acc[1] = cross

    @pl.when(t == B // PACE - 1)
    def _():
        rows = jnp.concatenate([to_row(acc[0]), to_row(acc[1])], axis=0)
        out_ref[...] = jnp.broadcast_to(rows[None], out_ref.shape)


def slope(stats, pre, cot, mask, gain, shift):
    return pl.pallas_call(
        slope_kernel,
        grid=(B // PACE,),
        in_specs=[
            whole(stats.shape),
            paced(),
            paced(),
            paced_mask(),
            whole((1, 128)),
            whole((1, 128)),
        ],
        out_specs=whole(stats.shape),
        out_shape=jax.ShapeDtypeStruct(stats.shape, F32),
        scratch_shapes=[pltpu.VMEM((4, C, 128), F32), pltpu.VMEM((2, C, 128), F32)],
        compiler_params=params(),
        name="slope",
    )(stats, pre, cot, mask, gain, shift)


def pre_grad_kernel(live_ref, stat_ref, stat2_ref, pre_ref, cot_ref, mask_ref, *refs):
    gain_ref, shift_ref, out_ref, small_ref = refs[:4]
    sides, (col_ref,) = refs[4:8], refs[8:]
    t = pl.program_id(0)
    ids = slots(live_ref)

    @pl.when(t == 0)
    def _():
        voxels, mean, inv = moments(stat_ref)
        total = jnp.sum(stat2_ref[...], axis=0)
        root = 1.0 / jnp.sqrt(voxels)
        small_ref[...] = jnp.zeros_like(small_ref)
        small_ref[0:1, :] = total[1:2, :] * root
        small_ref[1:2, :] = total[0:1, :] * root
        small_ref[2:3, :] = root
        gain = gain_ref[...]
        rows = (mean, inv, gain, shift_ref[...], gain * inv)
        rows = rows + (total[0:1, :] / voxels, total[1:2, :] / voxels)
        for k, row in enumerate(rows):
            col_ref[k] = jnp.broadcast_to(to_column(row), (C, 128))

    terms = [col_ref[k] for k in range(4)]
    scale, first, second = [col_ref[k] for k in range(4, 7)]
    for u in range(PACE):
        rows = slice(u * C, (u + 1) * C)
        tiles = []
        for k in range(4):
            lanes = slice(k * 128, (k + 1) * 128)
            normed, gz = slope_tile((pre_ref, cot_ref, mask_ref), u, k, terms)
            tile = (mask_ref[u][:, lanes] * scale * (gz - first - normed * second)).astype(BF16)
            out_ref[rows, lanes] = tile
            tiles.append(tile)
        emit_sides(PACE * t + u, tiles, ids, sides)


def pre_grad(live, stats, stats2, pre, cot, mask, gain, shift):
    return pl.pallas_call(
        pre_grad_kernel,
        grid=(B // PACE,),
        in_specs=[
            smem(),
            whole(stats.shape),
            whole(stats2.shape),
            paced(),
            paced(),
            paced_mask(),
            whole((1, 128)),
            whole((1, 128)),
        ],
        out_specs=[paced(), whole((8, 128))] + [whole(f.shape) for f in SIDES],
        out_shape=[
            jax.ShapeDtypeStruct((B * C, W2), BF16),
            jax.ShapeDtypeStruct((8, 128), F32),
        ]
        + SIDES,
        scratch_shapes=[pltpu.VMEM((7, C, 128), F32)],
        compiler_params=params(),
        name="pre_grad",
    )(live, stats, stats2, pre, cot, mask, gain, shift)


def weight_kernel(live_ref, body_ref, *refs):
    halo, (grad_ref, out_ref) = refs[:4], refs[4:6]
    edge_ref, rows_ref, cols_ref, padded, total = refs[6:]
    t = pl.program_id(0)

    @pl.when(t == 0)
    def _():
        padded[0 : 2 * C, :] = jnp.zeros((2 * C, W2), BF16)
        padded[2 * C : 18 * C, :] = grad_ref[...]
        padded[18 * C : ROWS, :] = jnp.zeros((2 * C, W2), BF16)
        total[...] = jnp.zeros_like(total)

    def use(i, cols):
        rows = pl.ds(i * C if isinstance(i, int) else pl.multiple_of(i * C, C), 3 * C)
        total[...] += lax.dot_general(
            padded[rows, :], cols[...], (((1,), (1,)), ((), ())), preferred_element_type=F32
        )

    run_planes(live_ref, body_ref, halo, edge_ref, rows_ref, cols_ref, use)

    @pl.when(t == 3)
    def _():
        for j in range(6):
            out_ref[j * 288 : (j + 1) * 288, :] = total[:, j * 128 : (j + 1) * 128]
        out_ref[6 * 288 : 2048, :] = jnp.zeros((2048 - 6 * 288, 128), F32)
        out_ref[6 * 288 : 7 * 288, 0:96] = total[:, 768:864]


def weight_terms(live, body, halo, grad):
    return pl.pallas_call(
        weight_kernel,
        grid=(4,),
        in_specs=[smem(), whole(body.shape)] + [whole(h) for h in HALO] + [whole(grad.shape)],
        out_specs=whole((2048, 128)),
        out_shape=jax.ShapeDtypeStruct((2048, 128), F32),
        scratch_shapes=ASSEMBLY
        + [pltpu.VMEM((ROWS, W2), BF16), pltpu.VMEM((3 * C, 9 * C), F32)],
        compiler_params=params(),
        name="weight_terms",
    )(live, body, *halo, grad)


def backward_kernel(live_ref, body_ref, *refs):
    halo, (weight_ref, mask_ref, out_ref) = refs[:4], refs[4:7]
    edge_ref, rows_ref, cols_ref, sums, spread = refs[7:]
    t = pl.program_id(0)

    @pl.when(t == 0)
    def _():
        ids = slots(live_ref)
        row, lane = iota((128, W2), 0), iota((128, W2), 1)
        start = jnp.where((row >> 6) == 0, ids[0], ids[1]) * B
        spread[...] = flags(
            (((row >> 4) & 3) == (lane >> 7)) & ((lane & 127) == start + (row & 15))
        )

    run_planes(
        live_ref, body_ref, halo, edge_ref, rows_ref, cols_ref, add_product(weight_ref, sums)
    )
    for u in range(4):
        rows = pl.ds(pl.multiple_of((4 * t + 2 + u) * C, C), C)
        mask = mask_ref[4 * t + u]
        for m in range(4):
            lanes = slice(m * 128, (m + 1) * 128)
            tile = (sums[rows, lanes] * mask[:, lanes]).astype(BF16)
            moved = jnp.dot(tile, spread[...], preferred_element_type=F32)
            for g in range(4):
                out_ref[u, 4 * g + m] = moved[:, g * 128 : (g + 1) * 128].astype(BF16)


def backward(live, body, halo, weight, mask):
    return pl.pallas_call(
        backward_kernel,
        grid=(4,),
        in_specs=[smem(), whole(body.shape)]
        + [whole(h) for h in HALO]
        + [whole(weight.shape), whole(mask.shape)],
        out_specs=pl.BlockSpec((4, B, C, 128), lambda t: (t, 0, 0, 0)),
        out_shape=jax.ShapeDtypeStruct((B, B, C, 128), BF16),
        scratch_shapes=ASSEMBLY + [pltpu.VMEM((ROWS, W2), F32), pltpu.VMEM((128, W2), BF16)],
        compiler_params=params(),
        name="backward",
    )(live, body, *halo, weight, mask)


def finish_kernel(sum_ref, small_ref, out_ref):
    base = pl.multiple_of((2 - pl.program_id(0)) * C, C)
    root = small_ref[2:3, 0:C]
    for k in range(9):
        start = k * C
        pieces = []
        while start < (k + 1) * C:
            j, off = start // 128, start % 128
            stop = min((k + 1) * C, (j + 1) * 128)
            rows = pl.ds(base + j * 288, C)
            pieces.append(sum_ref[rows, off : off + stop - start].astype(F32))
            start = stop
        block = pieces[0] if len(pieces) == 1 else jnp.concatenate(pieces, axis=1)
        out_ref[k] = block.T * root


def finish(sums, small):
    return pl.pallas_call(
        finish_kernel,
        grid=(3,),
        in_specs=[whole(sums.shape), whole(small.shape)],
        out_specs=pl.BlockSpec((9, C, C), lambda a: (a, 0, 0)),
        out_shape=jax.ShapeDtypeStruct((27, C, C), F32),
        compiler_params=params(),
        name="finish",
    )(sums, small)


def arrange_kernel(weight_ref, fwd_ref, back_ref):
    for a in range(3):
        for k in range(9):
            block = weight_ref[9 * a + k]
            fwd_ref[(2 - a) * C : (3 - a) * C, k * C : (k + 1) * C] = block.T
            back_ref[a * C : (a + 1) * C, (8 - k) * C : (9 - k) * C] = block


def arrange(weight):
    return pl.pallas_call(
        arrange_kernel,
        in_specs=[vmem()],
        out_specs=[vmem()] * 2,
        out_shape=[jax.ShapeDtypeStruct((3 * C, 9 * C), BF16)] * 2,
        compiler_params=params(),
        name="arrange",
    )(weight)


def swap_all(spread):
    return lax.all_to_all(spread, AXES, 0, 0, tiled=True)


def scatter_large(values):
    count = lax.axis_size("gx") * lax.axis_size("gy")
    parts = values.reshape(count, values.shape[0] // count, 128)
    return lax.all_to_all(parts, AXES, 0, 0, tiled=True)


def gather_large(parts):
    mine = jnp.sum(parts, axis=0)
    spread = jnp.broadcast_to(mine[None], parts.shape)
    return lax.all_to_all(spread, AXES, 0, 0, tiled=True).reshape(-1, 128)


def body(features, cotangent, weight, bn_gain, bn_shift, voxel_mask, brick_live):
    gain = jnp.pad(bn_gain, (0, 128 - C))[None]
    shift = jnp.pad(bn_shift, (0, 128 - C))[None]
    packed, mask, *sides = pack_features(brick_live, features, voxel_mask)
    weight_rows, weight_back = arrange(weight)
    halo, (weight_rows, weight_back) = exchange(sides, (weight_rows, weight_back))
    pre, stats = forward(brick_live, packed, halo, weight_rows, mask)
    cotangent, stats = lax.optimization_barrier((cotangent, stats))
    stats = swap_all(stats)
    cot = pack_plain(brick_live, cotangent)
    stats2 = slope(stats, pre, cot, mask, gain, shift)
    stats2 = swap_all(stats2)
    grad, small, *grad_sides = pre_grad(
        brick_live, stats, stats2, pre, cot, mask, gain, shift
    )
    terms = weight_terms(brick_live, packed, halo, grad)
    grad_halo, terms = exchange(grad_sides, terms)
    parts = scatter_large(terms)
    parts, grad_halo = lax.optimization_barrier((parts, grad_halo))
    sums = gather_large(parts)
    input_grad = backward(brick_live, grad, grad_halo, weight_back, mask)
    weight_grad = finish(sums, small)
    return input_grad, weight_grad, small[0, :C], small[1, :C]


def solution(mesh):
    return jax.shard_map(
        body,
        mesh=mesh,
        in_specs=(
            P("gx", "gy", None, None),
            P("gx", "gy", None, None),
            P(),
            P(),
            P(),
            P("gx", "gy", None),
            P("gx", "gy", None),
        ),
        out_specs=(P("gx", "gy", None, None), P(), P(), P()),
        check_vma=False,
    )
```

```python
import functools

import jax
import jax.numpy as jnp
from jax import lax
from jax.experimental import pallas as pl
from jax.experimental.pallas import tpu as pltpu
from jax.sharding import PartitionSpec as P

B = 16
C = 96
NB = 8
W2 = 512
ROWS = 20 * C
EDGE = C + 16
F32 = jnp.float32
BF16 = jnp.bfloat16
AXES = ("gx", "gy")


def params(mib=56):
    return pltpu.CompilerParams(vmem_limit_bytes=mib * 1024 * 1024)


def vmem():
    return pl.BlockSpec(memory_space=pltpu.VMEM)


def smem():
    return pl.BlockSpec(memory_space=pltpu.SMEM)


def iota(shape, dim):
    return lax.broadcasted_iota(jnp.int32, shape, dim)


def slots(live_ref):
    first = jnp.int32(-1)
    second = jnp.int32(-1)
    for j in reversed(range(NB)):
        on = live_ref[0, 0, j] > 0
        second = jnp.where(on, first, second)
        first = jnp.where(on, jnp.int32(j), first)
    first = jnp.maximum(first, 0)
    spare = jnp.bitwise_and(first + 1, NB - 1)
    return first, jnp.where(second >= 0, second, spare)


def wrap(shift):
    return jnp.bitwise_and(shift + 256, 127)


def lane_parts(shape):
    lane = iota(shape, 1)
    return lane >> 6, (lane >> 4) & 3, lane & 15


def scaled(tile, row):
    return (tile.reshape(C // 16, 16, 128) * row[None]).reshape(C, 128)


def flags(cond):
    return jnp.where(cond, 1.0, 0.0).astype(BF16)


def by_slot(first, second, shape=(16, 128)):
    return jnp.where(lane_parts(shape)[0] == 0, first, second)


def fill_selector(sel_ref, ids):
    row = iota((512, 128), 0)
    slot, group, deep = lane_parts((512, 128))
    start = jnp.where(slot == 0, ids[0], ids[1]) * B
    sel_ref[...] = flags(((row >> 7) == group) & ((row & 127) == start + deep))


def emit_sides(x, tiles, ids, sides):
    xa, xb, ya, yb = sides
    odd_x = lax.axis_index("gx") % 2
    odd_y = lax.axis_index("gy") % 2
    group = lane_parts((C, 128))[1]

    @pl.when(x == 0)
    def _():
        tag = by_slot(ids[0], ids[1]).astype(F32).astype(BF16)
        for face in sides:
            for k in range(4):
                face[C:EDGE, k * 128 : (k + 1) * 128] = tag

    for face, where in ((xa, jnp.where(odd_x == 1, 0, B - 1)), (xb, jnp.where(odd_x == 1, B - 1, 0))):

        @pl.when(x == where)
        def _(face=face):
            for k in range(4):
                face[0:C, k * 128 : (k + 1) * 128] = tiles[k]

    spot = x // 4
    lanes = pl.ds(pl.multiple_of(lax.rem(x, 4) * 128, 128), 128)
    low = pltpu.roll(tiles[0], wrap(16 * spot), 1)
    high = pltpu.roll(tiles[3], wrap(16 * spot - 48), 1)
    for face, flip in ((ya, 1), (yb, 0)):
        moved = jnp.where(odd_y == flip, low, high)
        face[0:C, lanes] = jnp.where(group == spot, moved, face[0:C, lanes])


SIDES = [jax.ShapeDtypeStruct((EDGE, W2), BF16)] * 4


PACE = 8


def paced():
    return pl.BlockSpec((PACE * C, W2), lambda t: (t, 0))


def paced_mask():
    return pl.BlockSpec((PACE, 1, W2), lambda t: (t, 0, 0))


def whole(shape):
    return pl.BlockSpec(shape, lambda *a: (0,) * len(shape))


def pack_features_kernel(live_ref, feat_ref, mask_ref, out_ref, live_out, *refs):
    sides, (sel_ref, lhs_ref) = refs[:4], refs[4:]
    t = pl.program_id(0)
    ids = slots(live_ref)

    @pl.when(t == 0)
    def _():
        fill_selector(sel_ref, ids)

    brick = iota((B, 128), 1) >> 4
    column = jnp.zeros((B, 128), F32)
    for j in range(NB):
        column = jnp.where(brick == j, live_ref[0, 0, j].astype(F32), column)
    for u in range(PACE):
        cells = mask_ref[u].astype(F32) * column
        for y in range(B):
            row = jnp.broadcast_to(cells[y : y + 1, :], (16, 128)).astype(BF16)
            base, lanes = (4 * u + y % 4) * EDGE, slice((y // 4) * 128, (y // 4 + 1) * 128)
            lhs_ref[base : base + C, lanes] = scaled(feat_ref[u, y], row)
            lhs_ref[base + C : base + EDGE, lanes] = row
    moved = jnp.dot(lhs_ref[...], sel_ref[...], preferred_element_type=F32)
    for u in range(PACE):
        tiles = []
        for m in range(4):
            lanes = slice(m * 128, (m + 1) * 128)
            base = (4 * u + m) * EDGE
            tile = moved[base : base + C].astype(BF16)
            out_ref[u * C : (u + 1) * C, lanes] = tile
            live_out[u, :, lanes] = moved[base + C : base + C + 1]
            tiles.append(tile)
        emit_sides(PACE * t + u, tiles, ids, sides)


def pack_features(live, features, mask):
    return pl.pallas_call(
        pack_features_kernel,
        grid=(B // PACE,),
        in_specs=[
            smem(),
            pl.BlockSpec((PACE, B, C, 128), lambda t: (t, 0, 0, 0)),
            pl.BlockSpec((PACE, B, 128), lambda t: (t, 0, 0)),
        ],
        out_specs=[paced(), paced_mask()]
        + [whole(f.shape) for f in SIDES],
        out_shape=[
            jax.ShapeDtypeStruct((B * C, W2), BF16),
            jax.ShapeDtypeStruct((B, 1, W2), F32),
        ]
        + SIDES,
        scratch_shapes=[pltpu.VMEM((512, 128), BF16), pltpu.VMEM((PACE * 4 * EDGE, 512), BF16)],
        compiler_params=params(),
        name="pack_features",
    )(live, features, mask)


def pack_plain_kernel(live_ref, feat_ref, out_ref, sel_ref, lhs_ref):
    ids = slots(live_ref)

    @pl.when(pl.program_id(0) == 0)
    def _():
        fill_selector(sel_ref, ids)

    for u in range(PACE):
        for y in range(B):
            base, lanes = (4 * u + y % 4) * C, slice((y // 4) * 128, (y // 4 + 1) * 128)
            lhs_ref[base : base + C, lanes] = feat_ref[u, y]
    moved = jnp.dot(lhs_ref[...], sel_ref[...], preferred_element_type=F32)
    for u in range(PACE):
        for m in range(4):
            base = (4 * u + m) * C
            out_ref[u * C : (u + 1) * C, m * 128 : (m + 1) * 128] = moved[base : base + C].astype(
                BF16
            )


def pack_plain(live, values):
    return pl.pallas_call(
        pack_plain_kernel,
        grid=(B // PACE,),
        in_specs=[smem(), pl.BlockSpec((PACE, B, C, 128), lambda t: (t, 0, 0, 0))],
        out_specs=paced(),
        out_shape=jax.ShapeDtypeStruct((B * C, W2), BF16),
        scratch_shapes=[pltpu.VMEM((512, 128), BF16), pltpu.VMEM((PACE * 4 * C, 512), BF16)],
        compiler_params=params(),
        name="pack_cotangent",
    )(live, values)


def pick(odd, first, second):
    return jnp.where(odd == 1, first, second), jnp.where(odd == 1, second, first)


def relay_kernel(xa, xb, ya, yb, ya_out, yb_out):
    odd_x = lax.axis_index("gx") % 2
    odd_y = lax.axis_index("gy") % 2
    group = lane_parts((EDGE, 128))[1]
    zero = jnp.zeros((EDGE, 128), BF16)
    edges = []
    for tile, turn in ((0, 0), (3, 80)):
        lanes = slice(tile * 128, (tile + 1) * 128)
        below, above = pick(odd_x, xa[:, lanes], xb[:, lanes])
        if turn:
            below = pltpu.roll(below, turn, 1)
        above = pltpu.roll(above, (turn + 16) % 128, 1)
        edges.append(jnp.where(group == 0, below, jnp.where(group == 1, above, zero)))
    high_first = jnp.where(odd_y == 1, edges[0], edges[1])
    low_first = jnp.where(odd_y == 1, edges[1], edges[0])
    ya_out[:, 0:W2] = ya[...]
    yb_out[:, 0:W2] = yb[...]
    ya_out[:, W2:640] = high_first
    yb_out[:, W2:640] = low_first


def relay(xa, xb, ya, yb):
    return pl.pallas_call(
        relay_kernel,
        in_specs=[vmem()] * 4,
        out_specs=[vmem()] * 2,
        out_shape=[jax.ShapeDtypeStruct((EDGE, 640), BF16)] * 2,
        compiler_params=params(),
        name="relay",
    )(xa, xb, ya, yb)


def swap(values, axis, first):
    count = lax.axis_size(axis)
    pairs = []
    for i in range(count):
        j = i ^ 1 if first else ((i + 1) ^ 1) - 1
        if 0 <= j < count:
            pairs.append((i, j))
    return lax.ppermute(values, axis, pairs)


def exchange(sides, beside, then):
    xa, xb, ya, yb = sides
    xa = swap(xa, "gx", True)
    xb = swap(xb, "gx", False)
    xa, xb, beside = lax.optimization_barrier((xa, xb, beside))
    ya, yb = relay(xa, xb, ya, yb)
    made = then(beside)
    ya = swap(ya, "gy", True)
    yb = swap(yb, "gy", False)
    ya, yb, made = lax.optimization_barrier((ya, yb, made))
    return (xa, xb, ya, yb), made


HALO = [(EDGE, W2), (EDGE, W2), (EDGE, 640), (EDGE, 640)]


class Columns:
    def __init__(self, ids, halo, edge_ref, rows_ref):
        self.halo, self.edge_ref, self.rows_ref = halo, edge_ref, rows_ref
        self.ids = ids
        slot, group, deep = lane_parts((16, 128))
        after = (ids[1] == ids[0] + 1) & (ids[1] > 0)
        near = jnp.where(after, 1, 0)
        self.keep_low = flags(deep > 0)
        self.keep_high = flags(deep < 15)
        self.at_low = flags(deep == 0)
        self.at_high = flags(deep == 15)
        self.from_next = flags((deep == 15) & (slot < near))
        self.from_last = flags((deep == 0) & (slot + near == 2))
        self.first = flags(group == 0)
        self.not_first = flags(group > 0)
        self.last = flags(group == 3)
        self.not_last = flags(group < 3)

    def prepare(self):
        xa, xb, ya, yb = self.halo
        odd_x = lax.axis_index("gx") % 2
        odd_y = lax.axis_index("gy") % 2
        mine = by_slot(self.ids[0], self.ids[1]).astype(F32)

        def shifted(cells):
            tag = cells[C:EDGE].astype(F32)
            turned = pltpu.roll(tag, 64, 1)
            body = cells[0:C]
            other = pltpu.roll(body, 64, 1)
            under, here, over = [
                scaled(body, flags(tag == mine + d)) + scaled(other, flags(turned == mine + d))
                for d in (-1.0, 0.0, 1.0)
            ]
            return (
                scaled(pltpu.roll(here, 1, 1), self.keep_low)
                + scaled(pltpu.roll(under, 113, 1), self.at_low),
                here,
                scaled(pltpu.roll(here, 127, 1), self.keep_high)
                + scaled(pltpu.roll(over, 15, 1), self.at_high),
            )

        def lanes(k):
            return slice(k * 128, (k + 1) * 128)

        for k in range(5):
            for way, cells in enumerate(pick(odd_y, ya[:, lanes(k)], yb[:, lanes(k)])):
                for dz, tile in enumerate(shifted(cells)):
                    self.rows_ref[way, dz, :, lanes(k)] = tile
        for k in range(4):
            for way, cells in enumerate(pick(odd_x, xa[:, lanes(k)], xb[:, lanes(k)])):
                for dz, tile in enumerate(shifted(cells)):
                    self.edge_ref[way, dz, :, lanes(k)] = tile

    def store(self, cols, dz, tiles, below, above):
        head = scaled(pltpu.roll(tiles[3], 16, 1), self.not_first) + scaled(below, self.first)
        tail = scaled(pltpu.roll(tiles[0], 112, 1), self.not_last) + scaled(above, self.last)
        line = [head] + list(tiles) + [tail]
        for dy in range(3):
            k = dy * 3 + dz
            for m in range(4):
                cols[k * C : (k + 1) * C, m * 128 : (m + 1) * 128] = line[dy + m]

    def edge(self, way, cols):
        for dz in range(3):
            tiles = [self.edge_ref[way, dz, :, m * 128 : (m + 1) * 128] for m in range(4)]
            low = self.rows_ref[0, dz, :, W2:640]
            high = self.rows_ref[1, dz, :, W2:640]
            self.store(
                cols,
                dz,
                tiles,
                pltpu.roll(low, 112, 1) if way else low,
                pltpu.roll(high, 32 if way else 48, 1),
            )

    def inner(self, x, body, cols):
        here = [body[:, m * 128 : (m + 1) * 128] for m in range(4)]
        spot = x // 4
        lanes = pl.ds(pl.multiple_of(lax.rem(x, 4) * 128, 128), 128)
        for dz in range(3):
            if dz == 0:
                tiles = [
                    scaled(pltpu.roll(t, 1, 1), self.keep_low)
                    + scaled(pltpu.roll(t, 49, 1), self.from_last)
                    for t in here
                ]
            elif dz == 1:
                tiles = here
            else:
                tiles = [
                    scaled(pltpu.roll(t, 127, 1), self.keep_high)
                    + scaled(pltpu.roll(t, 79, 1), self.from_next)
                    for t in here
                ]
            below = pltpu.roll(self.rows_ref[0, dz, :, lanes], wrap(-16 * spot), 1)
            above = pltpu.roll(self.rows_ref[1, dz, :, lanes], wrap(48 - 16 * spot), 1)
            self.store(cols, dz, tiles, below, above)


ASSEMBLY = [
    pltpu.VMEM((2, 3, C, W2), BF16),
    pltpu.VMEM((2, 3, C, 640), BF16),
    pltpu.VMEM((2, 9 * C, W2), BF16),
]


def run_planes(live_ref, body_ref, halo, edge_ref, rows_ref, cols_ref, use):
    t = pl.program_id(0)
    columns = Columns(slots(live_ref), halo, edge_ref, rows_ref)
    bufs = [cols_ref.at[k] for k in range(2)]

    def build(i, buf):
        if isinstance(i, int) and i in (0, 17):
            columns.edge(i // 17, buf)
        else:
            rows = (i - 1) * C
            if not isinstance(i, int):
                rows = pl.multiple_of(rows, C)
            columns.inner(i - 1, body_ref[pl.ds(rows, C), :], buf)

    def pass_over(base, count):
        for j in range(count):
            if not isinstance(base, int) or base + j < 17:
                build(base + j + 1, bufs[(j + 1) % 2])
            use(base + j, bufs[j % 2])

    @pl.when(t == 0)
    def _():
        columns.prepare()
        build(0, bufs[0])
        pass_over(0, 6)

    @pl.when((t > 0) & (t < 3))
    def _():
        pass_over(2 + 4 * t, 4)

    @pl.when(t == 3)
    def _():
        pass_over(14, 4)


def four_planes():
    return pl.BlockSpec((4 * C, W2), lambda t: (t, 0))


def fold(values):
    return (values[:, 0:128] + values[:, 128:256]) + (values[:, 256:384] + values[:, 384:512])


def to_row(column_tile):
    column = jnp.sum(column_tile, axis=1, keepdims=True)
    diag = iota((C, 128), 0) == iota((C, 128), 1)
    return jnp.sum(jnp.where(diag, column, 0.0), axis=0, keepdims=True)


def to_column(row):
    diag = iota((C, 128), 0) == iota((C, 128), 1)
    return jnp.sum(jnp.where(diag, row, 0.0), axis=1, keepdims=True)


def add_product(weight_ref, sums):
    def use(i, cols):
        part = jnp.dot(weight_ref[...], cols[...], preferred_element_type=F32)
        rows = i * C if isinstance(i, int) else pl.multiple_of(i * C, C)
        sums[pl.ds(rows, 2 * C), :] += part[0 : 2 * C]
        sums[pl.ds(rows + 2 * C, C), :] = part[2 * C : 3 * C]

    return use


def forward_kernel(live_ref, body_ref, *refs):
    halo, (weight_ref, mask_ref, pre_ref, stat_ref) = refs[:4], refs[4:8]
    edge_ref, rows_ref, cols_ref, sums, acc = refs[8:]
    t = pl.program_id(0)

    @pl.when(t == 0)
    def _():
        acc[...] = jnp.zeros_like(acc)

    run_planes(
        live_ref, body_ref, halo, edge_ref, rows_ref, cols_ref, add_product(weight_ref, sums)
    )
    for u in range(4):
        values = sums[pl.ds(pl.multiple_of((4 * t + 2 + u) * C, C), C), :]
        mask = mask_ref[4 * t + u]
        held = values * mask
        pre_ref[u * C : (u + 1) * C, :] = values
        acc[0] += fold(held)
        acc[1] += fold(held * values)
        acc[2, 0:1, :] += fold(mask)

    @pl.when(t == 3)
    def _():
        lane = iota((1, 128), 1)
        total = jnp.where(lane == C, jnp.sum(acc[2, 0:1, :]), to_row(acc[0]))
        rows = jnp.concatenate([total, to_row(acc[1])], axis=0)
        stat_ref[...] = jnp.broadcast_to(rows[None], stat_ref.shape)


def devices():
    return lax.axis_size("gx") * lax.axis_size("gy")


def forward(live, body, halo, weight, mask):
    spread = (devices(), 2, 128)
    return pl.pallas_call(
        forward_kernel,
        grid=(4,),
        in_specs=[smem(), whole(body.shape)]
        + [whole(h) for h in HALO]
        + [whole(weight.shape), whole(mask.shape)],
        out_specs=[four_planes(), whole(spread)],
        out_shape=[
            jax.ShapeDtypeStruct((B * C, W2), F32),
            jax.ShapeDtypeStruct(spread, F32),
        ],
        scratch_shapes=ASSEMBLY + [pltpu.VMEM((ROWS, W2), F32), pltpu.VMEM((3, C, 128), F32)],
        compiler_params=params(),
        name="forward",
    )(live, body, *halo, weight, mask)


def moments(stat_ref):
    total = jnp.sum(stat_ref[...], axis=0)
    lane = iota((1, 128), 1)
    voxels = jnp.sum(jnp.where(lane == C, total[0:1, :], 0.0), axis=1, keepdims=True)
    voxels = jnp.broadcast_to(voxels, (1, 128))
    mean = total[0:1, :] / voxels
    var = total[1:2, :] / voxels - mean * mean
    return voxels, mean, lax.rsqrt(var + 1e-05)


def slope_tile(refs, u, k, terms):
    pre_ref, cot_ref, mask_ref = refs
    mean, inv, gain, shift = terms
    rows, lanes = slice(u * C, (u + 1) * C), slice(k * 128, (k + 1) * 128)
    normed = (pre_ref[rows, lanes] - mean) * inv
    zed = gain * normed + shift
    sig = 0.5 + 0.5 * jnp.tanh(0.5 * zed)
    held = mask_ref[u][:, lanes] * cot_ref[rows, lanes].astype(F32)
    return normed, held * (sig * (1.0 + zed * (1.0 - sig)))


def slope_kernel(
    stat_ref, pre_ref, cot_ref, mask_ref, gain_ref, shift_ref, out_ref, col_ref, acc
):
    t = pl.program_id(0)

    @pl.when(t == 0)
    def _():
        voxels, mean, inv = moments(stat_ref)
        for k, row in enumerate((mean, inv, gain_ref[...], shift_ref[...])):
            col_ref[k] = jnp.broadcast_to(to_column(row), (C, 128))
        acc[...] = jnp.zeros_like(acc)

    terms = [col_ref[k] for k in range(4)]
    total = acc[0]
    cross = acc[1]
    for u in range(PACE):
        for k in range(4):
            normed, gz = slope_tile((pre_ref, cot_ref, mask_ref), u, k, terms)
            total += gz
            cross += gz * normed
    acc[0] = total
    acc[1] = cross

    @pl.when(t == B // PACE - 1)
    def _():
        rows = jnp.concatenate([to_row(acc[0]), to_row(acc[1])], axis=0)
        out_ref[...] = jnp.broadcast_to(rows[None], out_ref.shape)


def slope(stats, pre, cot, mask, gain, shift):
    return pl.pallas_call(
        slope_kernel,
        grid=(B // PACE,),
        in_specs=[
            whole(stats.shape),
            paced(),
            paced(),
            paced_mask(),
            whole((1, 128)),
            whole((1, 128)),
        ],
        out_specs=whole(stats.shape),
        out_shape=jax.ShapeDtypeStruct(stats.shape, F32),
        scratch_shapes=[pltpu.VMEM((4, C, 128), F32), pltpu.VMEM((2, C, 128), F32)],
        compiler_params=params(),
        name="slope",
    )(stats, pre, cot, mask, gain, shift)


def pre_grad_kernel(live_ref, stat_ref, stat2_ref, pre_ref, cot_ref, mask_ref, *refs):
    gain_ref, shift_ref, out_ref, small_ref = refs[:4]
    sides, (col_ref,) = refs[4:8], refs[8:]
    t = pl.program_id(0)
    ids = slots(live_ref)

    @pl.when(t == 0)
    def _():
        voxels, mean, inv = moments(stat_ref)
        total = jnp.sum(stat2_ref[...], axis=0)
        root = 1.0 / jnp.sqrt(voxels)
        small_ref[...] = jnp.zeros_like(small_ref)
        small_ref[0:1, :] = total[1:2, :] * root
        small_ref[1:2, :] = total[0:1, :] * root
        small_ref[2:3, :] = root
        gain = gain_ref[...]
        rows = (mean, inv, gain, shift_ref[...], gain * inv)
        rows = rows + (total[0:1, :] / voxels, total[1:2, :] / voxels)
        for k, row in enumerate(rows):
            col_ref[k] = jnp.broadcast_to(to_column(row), (C, 128))

    terms = [col_ref[k] for k in range(4)]
    scale, first, second = [col_ref[k] for k in range(4, 7)]
    for u in range(PACE):
        rows = slice(u * C, (u + 1) * C)
        tiles = []
        for k in range(4):
            lanes = slice(k * 128, (k + 1) * 128)
            normed, gz = slope_tile((pre_ref, cot_ref, mask_ref), u, k, terms)
            tile = (mask_ref[u][:, lanes] * scale * (gz - first - normed * second)).astype(BF16)
            out_ref[rows, lanes] = tile
            tiles.append(tile)
        emit_sides(PACE * t + u, tiles, ids, sides)


def pre_grad(live, stats, stats2, pre, cot, mask, gain, shift):
    return pl.pallas_call(
        pre_grad_kernel,
        grid=(B // PACE,),
        in_specs=[
            smem(),
            whole(stats.shape),
            whole(stats2.shape),
            paced(),
            paced(),
            paced_mask(),
            whole((1, 128)),
            whole((1, 128)),
        ],
        out_specs=[paced(), whole((8, 128))] + [whole(f.shape) for f in SIDES],
        out_shape=[
            jax.ShapeDtypeStruct((B * C, W2), BF16),
            jax.ShapeDtypeStruct((8, 128), F32),
        ]
        + SIDES,
        scratch_shapes=[pltpu.VMEM((7, C, 128), F32)],
        compiler_params=params(),
        name="pre_grad",
    )(live, stats, stats2, pre, cot, mask, gain, shift)


def weight_kernel(pairs, live_ref, body_ref, *refs):
    halo, (grad_ref, mine_ref, other_ref) = refs[:4], refs[4:7]
    edge_ref, rows_ref, cols_ref, padded, total, line = refs[7:]
    t = pl.program_id(0)

    @pl.when(t == 0)
    def _():
        padded[0 : 2 * C, :] = jnp.zeros((2 * C, W2), BF16)
        padded[2 * C : 18 * C, :] = grad_ref[...]
        padded[18 * C : ROWS, :] = jnp.zeros((2 * C, W2), BF16)
        total[...] = jnp.zeros_like(total)

    def use(i, cols):
        rows = pl.ds(i * C if isinstance(i, int) else pl.multiple_of(i * C, C), 3 * C)
        total[...] += lax.dot_general(
            padded[rows, :], cols[...], (((1,), (1,)), ((), ())), preferred_element_type=F32
        )

    run_planes(live_ref, body_ref, halo, edge_ref, rows_ref, cols_ref, use)

    @pl.when(t == 3)
    def _():
        for j in range(6):
            line[j * 288 : (j + 1) * 288, :] = total[:, j * 128 : (j + 1) * 128]
        line[6 * 288 : 2048, :] = jnp.zeros((2048 - 6 * 288, 128), F32)
        line[6 * 288 : 7 * 288, 0:96] = total[:, 768:864]
        odd = lax.axis_index("gx") % 2
        span = mine_ref.shape[0] // pairs
        for a in range(pairs):
            for ref, k in ((mine_ref, odd), (other_ref, 1 - odd)):
                rows = pl.ds(pl.multiple_of((2 * a + k) * span, span), span)
                ref[a * span : (a + 1) * span, :] = line[rows, :]


def weight_terms(live, body, halo, grad):
    return pl.pallas_call(
        functools.partial(weight_kernel, lax.axis_size("gx") // 2),
        grid=(4,),
        in_specs=[smem(), whole(body.shape)] + [whole(h) for h in HALO] + [whole(grad.shape)],
        out_specs=[whole((1024, 128))] * 2,
        out_shape=[jax.ShapeDtypeStruct((1024, 128), F32)] * 2,
        scratch_shapes=ASSEMBLY
        + [pltpu.VMEM((ROWS, W2), BF16), pltpu.VMEM((3 * C, 9 * C), F32), pltpu.VMEM((2048, 128), F32)],
        compiler_params=params(),
        name="weight_terms",
    )(live, body, *halo, grad)


def backward_kernel(live_ref, body_ref, *refs):
    halo, (weight_ref, mask_ref, out_ref) = refs[:4], refs[4:7]
    edge_ref, rows_ref, cols_ref, sums, spread = refs[7:]
    t = pl.program_id(0)

    @pl.when(t == 0)
    def _():
        ids = slots(live_ref)
        row, lane = iota((128, W2), 0), iota((128, W2), 1)
        start = jnp.where((row >> 6) == 0, ids[0], ids[1]) * B
        spread[...] = flags(
            (((row >> 4) & 3) == (lane >> 7)) & ((lane & 127) == start + (row & 15))
        )

    run_planes(
        live_ref, body_ref, halo, edge_ref, rows_ref, cols_ref, add_product(weight_ref, sums)
    )
    for u in range(4):
        rows = pl.ds(pl.multiple_of((4 * t + 2 + u) * C, C), C)
        mask = mask_ref[4 * t + u]
        for m in range(4):
            lanes = slice(m * 128, (m + 1) * 128)
            tile = (sums[rows, lanes] * mask[:, lanes]).astype(BF16)
            moved = jnp.dot(tile, spread[...], preferred_element_type=F32)
            for g in range(4):
                out_ref[u, 4 * g + m] = moved[:, g * 128 : (g + 1) * 128].astype(BF16)


def backward(live, body, halo, weight, mask):
    return pl.pallas_call(
        backward_kernel,
        grid=(4,),
        in_specs=[smem(), whole(body.shape)]
        + [whole(h) for h in HALO]
        + [whole(weight.shape), whole(mask.shape)],
        out_specs=pl.BlockSpec((4, B, C, 128), lambda t: (t, 0, 0, 0)),
        out_shape=jax.ShapeDtypeStruct((B, B, C, 128), BF16),
        scratch_shapes=ASSEMBLY + [pltpu.VMEM((ROWS, W2), F32), pltpu.VMEM((128, W2), BF16)],
        compiler_params=params(),
        name="backward",
    )(live, body, *halo, weight, mask)


def finish_kernel(sum_ref, small_ref, out_ref, gain_out, shift_out):
    gain_out[...] = small_ref[0:1, 0:C]
    shift_out[...] = small_ref[1:2, 0:C]
    base = pl.multiple_of((2 - pl.program_id(0)) * C, C)
    root = small_ref[2:3, 0:C]
    for k in range(9):
        start = k * C
        pieces = []
        while start < (k + 1) * C:
            j, off = start // 128, start % 128
            stop = min((k + 1) * C, (j + 1) * 128)
            rows = pl.ds(base + j * 288, C)
            pieces.append(sum_ref[rows, off : off + stop - start].astype(F32))
            start = stop
        block = pieces[0] if len(pieces) == 1 else jnp.concatenate(pieces, axis=1)
        out_ref[k] = block.T * root


def finish(sums, small):
    return pl.pallas_call(
        finish_kernel,
        grid=(3,),
        in_specs=[whole(sums.shape), whole(small.shape)],
        out_specs=[pl.BlockSpec((9, C, C), lambda a: (a, 0, 0)), whole((1, C)), whole((1, C))],
        out_shape=[jax.ShapeDtypeStruct((27, C, C), F32)]
        + [jax.ShapeDtypeStruct((1, C), F32)] * 2,
        compiler_params=params(),
        name="finish",
    )(sums, small)


def arrange_kernel(weight_ref, fwd_ref, back_ref):
    for a in range(3):
        for k in range(9):
            block = weight_ref[9 * a + k]
            fwd_ref[(2 - a) * C : (3 - a) * C, k * C : (k + 1) * C] = block.T
            back_ref[a * C : (a + 1) * C, (8 - k) * C : (9 - k) * C] = block


def arrange(weight):
    return pl.pallas_call(
        arrange_kernel,
        in_specs=[vmem()],
        out_specs=[vmem()] * 2,
        out_shape=[jax.ShapeDtypeStruct((3 * C, 9 * C), BF16)] * 2,
        compiler_params=params(),
        name="arrange",
    )(weight)


def swap_all(spread):
    return lax.all_to_all(spread, AXES, 0, 0, tiled=True)


def sum_pair(terms):
    mine, other = terms
    return scatter_large(mine + swap(other, "gx", True))


def scatter_large(mine):
    nx, ny = lax.axis_size("gx"), lax.axis_size("gy")
    groups = [[i * ny + j for i in range(c, nx, 2) for j in range(ny)] for c in range(2)]
    count = nx * ny // 2
    parts = mine.reshape(count, mine.shape[0] // count, 128)
    return lax.all_to_all(parts, AXES, 0, 0, tiled=True, axis_index_groups=groups)


def gather_large(parts):
    mine = jnp.sum(parts, axis=0).astype(BF16)
    spread = jnp.broadcast_to(mine[None], (devices(),) + mine.shape)
    return lax.all_to_all(spread, AXES, 0, 0, tiled=True).reshape(-1, 128)


def body(features, cotangent, weight, bn_gain, bn_shift, voxel_mask, brick_live):
    gain = jnp.pad(bn_gain, (0, 128 - C))[None]
    shift = jnp.pad(bn_shift, (0, 128 - C))[None]
    packed, mask, *sides = pack_features(brick_live, features, voxel_mask)
    weight_rows, weight_back = arrange(weight)
    cot = pack_plain(brick_live, cotangent)
    halo, ((weight_rows, weight_back), cot) = exchange(
        sides, (weight_rows, weight_back), lambda beside: (beside, cot)
    )
    pre, stats = forward(brick_live, packed, halo, weight_rows, mask)
    stats = swap_all(stats)
    stats2 = slope(stats, pre, cot, mask, gain, shift)
    stats2 = swap_all(stats2)
    grad, small, *grad_sides = pre_grad(
        brick_live, stats, stats2, pre, cot, mask, gain, shift
    )
    terms = weight_terms(brick_live, packed, halo, grad)
    grad_halo, parts = exchange(grad_sides, terms, sum_pair)
    sums = gather_large(parts)
    input_grad = backward(brick_live, grad, grad_halo, weight_back, mask)
    weight_grad, gain_grad, shift_grad = finish(sums, small)
    return input_grad, weight_grad, gain_grad.reshape(C), shift_grad.reshape(C)


def solution(mesh):
    return jax.shard_map(
        body,
        mesh=mesh,
        in_specs=(
            P("gx", "gy", None, None),
            P("gx", "gy", None, None),
            P(),
            P(),
            P(),
            P("gx", "gy", None),
            P("gx", "gy", None),
        ),
        out_specs=(P("gx", "gy", None, None), P(), P(), P()),
        check_vma=False,
    )
```
